128 devices in a mesh: fsdp: 2 (over core), dp: 64 (over z, y, x).
Axes of the slice: x: 4, y: 4, z: 4, core: 2. Of those that a mesh axis runs over, the one named last changes fastest.
Arguments:
- grad_parts: bfloat16 [64, 8, 64, 8, 512], P('dp', None, None, 'fsdp'), may hold values from -0.1875 to 0.1875
- slot_block: int32 [2, 8], replicated, may hold values from -1 to 7, as said below
- gram_left: float32 [16, 512, 512], P('fsdp', 'dp'), may hold values from -1.2 to 1.2
- gram_right: float32 [16, 512, 512], P('fsdp', 'dp'), may hold values from -1.2 to 1.2
- left_basis_t: bfloat16 [16, 512, 512], P('fsdp', 'dp'), may hold values from -0.25 to 0.25
- right_basis: bfloat16 [16, 512, 512], P('fsdp', 'dp'), may hold values from -0.25 to 0.25
- moment_first: float32 [16, 512, 512], P('fsdp', 'dp'), may hold values from -0.3 to 0.3
- moment_second: float32 [16, 512, 512], P('fsdp', 'dp'), may hold values from 0.002 to 0.05
Outputs:
- gram_left_new: float32 [16, 512, 512], P('fsdp', 'dp')
- gram_right_new: float32 [16, 512, 512], P('fsdp', 'dp')
- moment_first_new: float32 [16, 512, 512], P('fsdp', 'dp')
- moment_second_new: float32 [16, 512, 512], P('fsdp', 'dp')
- direction: bfloat16 [8, 64, 8, 512], P(None, 'dp', 'fsdp')
The draws below stay inside these ranges and needn't reach their ends.
Inputs may be any that keep to these rules, and one draw needn't show every extreme that they name: `slot_block`: every block 0 to 7 stands in exactly one slot; an owner's filled slots come first and the rest hold -1; some owner has all 8 slots filled.
All inputs are finite; a program needn't handle non-finite values.
Results may differ from the reference program's by a relative error of at most 0.0065.
Values may be sent and summed in bfloat16 or wider, within the bound.
No kernel may reach another device: no remote copies, remote signals or barrier semaphores. Data moves between devices by JAX's collectives and lax.ppermute only.
A program may use at most 64 MiB of HBM per device.

```python
import math
import jax
import jax.numpy as jnp
from jax import lax

BS = 512
CAP = 8
NBLK = 8
SLOTS = 16
N_FSDP = 2
N_DP = 64


def draw_slot_block(key, part):
    key = jax.random.fold_in(key, 7)
    key_split, key_owner, key_block = jax.random.split(key, 3)
    pair_count = N_FSDP // 2
    split_point = jax.random.randint(key_split, (pair_count,), 0, CAP + 1)
    split_point = split_point.at[0].set(CAP)
    pair_loads = jnp.stack([split_point, CAP - split_point], axis=1).reshape(N_FSDP)
    owner_order = jax.random.permutation(key_owner, N_FSDP)
    loads = jnp.zeros((N_FSDP,), jnp.int32).at[owner_order].set(pair_loads.astype(jnp.int32))
    first_slot = jnp.cumsum(loads) - loads
    block_order = jax.random.permutation(key_block, NBLK).astype(jnp.int32)
    slot_index = jnp.arange(CAP, dtype=jnp.int32)
    position = first_slot[:, None] + slot_index[None, :]
    filled = slot_index[None, :] < loads[:, None]
    table = jnp.where(filled, block_order[jnp.minimum(position, NBLK - 1)], -1)
    return table.astype(jnp.int32)


def spiked(drawn, own_key, source, target, parts, factor):
    def block_of(axis_at):
        return (jnp.arange(drawn.shape[axis_at]) // (drawn.shape[axis_at] // parts)).reshape((-1,) + (1,) * (drawn.ndim - 1 - axis_at))

    one_side = jax.random.permutation(own_key, parts)[block_of(target)]
    second = (block_of(target) + parts // 2) % parts
    return jnp.where((block_of(source) == one_side) | (block_of(source) == second), factor * drawn, drawn)


def shard_levels(stream_key, dims, cuts, low, largest):
    factor_of, own = 1.0, jax.random.fold_in(stream_key, 6)
    for axis_at, parts in cuts:
        draws = jnp.exp(jax.random.uniform(jax.random.fold_in(own, axis_at), (parts,), jnp.float32, low / len(cuts), largest / len(cuts)))
        factor_of = factor_of * jnp.repeat(draws, dims[axis_at] // parts).reshape([-1 if axis == axis_at else 1 for axis in range(len(dims))])
    return factor_of


def bell_draw(own_key, extent, spread, limit, cuts=(), held_as=jnp.bfloat16):
    entries = jax.random.normal(own_key, extent, jnp.float32) * spread
    if len(cuts) > 0:
        entries = shard_levels(own_key, extent, cuts, -0.22, 0.18) * entries
    return jnp.clip(entries, min=-limit, max=limit).astype(held_as)


def gaussian_with(own_key, dims, deviation, most, shards, heavy, kind=jnp.bfloat16):
    entries = deviation * jax.random.normal(own_key, dims, jnp.float32)
    if shards:
        entries = entries * shard_levels(own_key, dims, shards, -0.22, 0.18)
    return jnp.clip(spiked(entries, jax.random.fold_in(own_key, 3), *heavy), -most, most).astype(kind)


def setup_inputs(seed: int = 0) -> dict:
    key_of = jax.random.split(jax.random.key(seed), 9)
    grad_parts = gaussian_with(key_of[0], (N_DP, NBLK, N_DP, BS // N_DP, BS), (2.0 / (BS * N_DP) ** 0.5), 0.1875, ((0, 64), (3, 2)), (0, 2, 64, 4.0))
    slot_block = draw_slot_block(jax.random.fold_in(key_of[8], 71), 0)
    gram_left = bell_draw(key_of[2], (SLOTS, BS, BS), 0.2, 1.2, ((0, 2), (1, 64)), jnp.float32)
    gram_right = bell_draw(key_of[3], (SLOTS, BS, BS), 0.2, 1.2, ((0, 2), (1, 64)), jnp.float32)
    left_basis_t = bell_draw(key_of[4], (SLOTS, BS, BS), BS ** -0.5, 0.25, ((0, 2), (1, 64)))
    right_basis = bell_draw(key_of[5], (SLOTS, BS, BS), BS ** -0.5, 0.25, ((0, 2), (1, 64)))
    moment_first = bell_draw(key_of[6], (SLOTS, BS, BS), 0.05, 0.3, ((0, 2), (1, 64)), jnp.float32)
    moment_second = jnp.clip(jnp.exp(math.log(0.05) - 3.218876 * jax.random.uniform(key_of[7], (SLOTS, BS, BS), jnp.float32) ** shard_levels(key_of[7], (SLOTS, BS, BS), ((0, 2), (1, 64)), -0.2, 0.2)), 0.002, 0.05)
    return dict(grad_parts=grad_parts, slot_block=slot_block, gram_left=gram_left, gram_right=gram_right, left_basis_t=left_basis_t, right_basis=right_basis, moment_first=moment_first, moment_second=moment_second)


shampoo_beta = 0.9
adam_first = 0.95
adam_second = 0.95
epsilon = 1e-08

def update_slot(packed):
    block, gram_l, gram_r, basis_lt, basis_r, first, second = packed
    gram_l_new = shampoo_beta * gram_l + (1.0 - shampoo_beta) * jnp.dot(block, block.T, preferred_element_type=jnp.float32)
    gram_r_new = shampoo_beta * gram_r + (1.0 - shampoo_beta) * jnp.dot(block.T, block, preferred_element_type=jnp.float32)
    half_rot = jnp.dot(basis_lt, block, preferred_element_type=jnp.float32).astype(jnp.bfloat16)
    rotated = jnp.dot(half_rot, basis_r, preferred_element_type=jnp.float32)
    first_new = adam_first * first + (1.0 - adam_first) * rotated
    second_new = adam_second * second + (1.0 - adam_second) * rotated * rotated
    scaled = (first_new / (jnp.sqrt(second_new) + epsilon)).astype(jnp.bfloat16)
    back_right = jnp.dot(scaled, basis_r.T, preferred_element_type=jnp.float32).astype(jnp.bfloat16)
    slot_update = jnp.dot(basis_lt.T, back_right, preferred_element_type=jnp.float32).astype(jnp.bfloat16)
    return (gram_l_new, gram_r_new, first_new, second_new, slot_update)

def reference(grad_parts, slot_block, gram_left, gram_right, left_basis_t, right_basis, moment_first, moment_second):
    summed = lax.optimization_barrier(jnp.sum(grad_parts.astype(jnp.float32), axis=0))
    grads = summed.reshape(NBLK, BS, BS).astype(jnp.bfloat16)
    flat_slots = slot_block.reshape(-1).astype(jnp.int32)
    present = flat_slots >= 0
    chosen = grads[jnp.maximum(flat_slots, 0)]
    blocks = jnp.where(present[:, None, None], chosen, jnp.zeros((), chosen.dtype))
    gram_l_new, gram_r_new, first_new, second_new, updates = lax.map(update_slot, (blocks, gram_left, gram_right, left_basis_t, right_basis, moment_first, moment_second))
    target = jnp.where(present, flat_slots, NBLK).astype(jnp.int32)
    placed = jnp.zeros((NBLK, BS, BS), updates.dtype).at[target].set(updates, mode='drop')
    direction = placed.reshape(NBLK, N_DP, BS // N_DP, BS)
    return (gram_l_new, gram_r_new, first_new, second_new, direction)
```

```python
import jax
import jax.numpy as jnp
from jax import lax
from jax.experimental import pallas as pl
from jax.experimental.pallas import tpu as pltpu
from jax.sharding import PartitionSpec as P

shampoo_beta = 0.9
adam_first = 0.95
adam_second = 0.95
epsilon = 1e-08

GROUP = 8
AXES = ("fsdp", "dp")


def number(dp):
    b = g = 0
    for axis in range(3):
        place = (dp >> (2 * axis)) & 3
        wrap, inner = place >> 1, (place ^ (place >> 1)) & 1
        b += (inner if axis == 0 else wrap) << axis
        g += (wrap if axis == 0 else inner) << axis
    return b, g


PLACE = {number(dp): dp for dp in range(GROUP * GROUP)}
EIGHT = range(GROUP)


def device(c, b, g):
    return c * GROUP * GROUP + PLACE[b, g]


OVER_B = [[[device(c, b, g) for b in EIGHT] for g in EIGHT] for c in range(2)]
OVER_G = [[[device(c, b, g) for g in EIGHT] for b in EIGHT] for c in range(2)]
FIRST = OVER_B[0] + OVER_G[1]
SECOND = OVER_G[0] + OVER_B[1]
BLOCK = OVER_G[0] + OVER_G[1]
ALL = [[device(c, b, g) for b in EIGHT for g in EIGHT] for c in range(2)]


def exchange(x, groups):
    return lax.all_to_all(x, AXES, 0, 0, axis_index_groups=groups, tiled=True)


def swap_cores(x):
    return lax.ppermute(x, "fsdp", [(0, 1), (1, 0)])


def dot(a, b, ca=1, cb=0):
    return lax.dot_general(a, b, (((ca,), (cb,)), ((), ())), preferred_element_type=jnp.float32)


def iota(shape, axis):
    return lax.broadcasted_iota(jnp.int32, shape, axis)


def one_hot(hit):
    return jnp.where(hit, 1.0, 0.0).astype(jnp.bfloat16)


WHOLE = pl.BlockSpec(memory_space=pltpu.VMEM)
SCALARS = pl.BlockSpec(memory_space=pltpu.SMEM)
FAR = pl.BlockSpec(memory_space=pltpu.HBM)


def local_call(kernel, name, out_shape, in_specs, scratch=(), vmem=40, out=WHOLE):
    return pl.pallas_call(
        kernel,
        out_shape=out_shape,
        in_specs=in_specs,
        out_specs=jax.tree.map(lambda _: out, out_shape),
        scratch_shapes=list(scratch),
        compiler_params=pltpu.CompilerParams(vmem_limit_bytes=vmem * 2**20),
        name=name,
    )


def chain_kernel(raw, swapped, right, left_t, first, second, out):
    bf16 = jnp.bfloat16
    core = lax.axis_index("fsdp")
    lane = number(lax.axis_index("dp"))[1]
    size = raw.shape[1]
    picks = size // 8

    n = iota((256, 256), 0)
    at = ((n >> 2) & 1) * 128 + (n >> 6) * 32 + ((n >> 3) & 7) * 4 + (n & 3)
    pick = one_hot(iota((256, 256), 1) == at)
    low = jnp.where(core == 0, raw[...], swapped[...])
    high = jnp.where(core == 0, swapped[...], raw[...])
    block = []
    for i in range(0, size // 2, 128):
        rows = jnp.concatenate([low[i : i + 128], high[i : i + 128]], axis=0)
        block.append(dot(pick, rows).astype(bf16))
    block = jnp.concatenate(block, axis=0)

    half_rot = dot(left_t[...], block).astype(bf16)
    rotated = dot(half_rot, right[...])
    new_first = adam_first * first[...] + (1.0 - adam_first) * rotated
    new_second = adam_second * second[...] + (1.0 - adam_second) * rotated * rotated
    scaled = (new_first / (jnp.sqrt(new_second) + epsilon)).astype(bf16)
    back = dot(scaled, right[...], 1, 1).astype(bf16)
    update = dot(left_t[...], back, 0, 0)

    own = one_hot(iota((picks, size), 1) == iota((picks, size), 0) * 8 + lane)
    gram_l = dot(dot(own, block).astype(bf16), block, 1, 1).astype(bf16)
    gram_r = dot(dot(block, own, 1, 1).astype(bf16), block, 0, 0).astype(bf16)

    upper = rotated.astype(bf16)
    lower = (rotated - upper.astype(jnp.float32)).astype(bf16)
    rows = jnp.concatenate([gram_l, gram_r, upper, lower], axis=0)
    n, col = iota((size, 4 * picks), 0), iota((size, 4 * picks), 1)
    spread = one_hot(col == ((n & 7) - 4 * (1 - core)) * picks + (n >> 3))
    kept = (iota((size, size), 0) & 4) == 4 * core
    result = jnp.where(kept, update, dot(spread, rows))
    order = [PLACE[b, g] * 8 for b in EIGHT for g in EIGHT]
    out[...] = jnp.concatenate([result[at : at + 8] for at in order], axis=0).astype(bf16)


def chain(raw, *others):
    width = raw.shape[1]
    out = jax.ShapeDtypeStruct((width, width), jnp.bfloat16)
    return local_call(chain_kernel, "block_chain", out, [WHOLE] * 6)(raw, *others)


def finish_kernel(slot_block, home, gram_l, gram_r, first, second, *outs):
    gram_l_new, gram_r_new, first_new, second_new, direction = outs
    core = lax.axis_index("fsdp")
    n, col = iota((32, 64), 0), iota((32, 64), 1)
    kind, chip, row = n >> 3, col >> 3, col & 7
    other = row - 4 * (1 - core)
    product = (chip == (n & 7)) & ((other == kind) | ((kind == 2) & (other == 3)))
    hit = ((kind == 3) & (row - 4 * core == (n & 7))) | ((kind < 3) & product)
    take = one_hot(hit)
    for b in range(home.shape[0]):
        direction[b] = dot(take[24:], home[b])[:4].astype(jnp.bfloat16)
    share = jnp.where(slot_block[core, 0] >= 0, 1.0, 0.0)
    for slot in range(home.shape[0]):
        block = jnp.maximum(slot_block[core, slot], 0)
        rows = dot(take, home[block]) * share
        rotated = rows[16:24]
        gram_l_new[slot] = shampoo_beta * gram_l[slot] + (1.0 - shampoo_beta) * rows[:8]
        gram_r_new[slot] = shampoo_beta * gram_r[slot] + (1.0 - shampoo_beta) * rows[8:16]
        first_new[slot] = adam_first * first[slot] + (1.0 - adam_first) * rotated
        second_new[slot] = (
            adam_second * second[slot] + (1.0 - adam_second) * rotated * rotated
        )


def finish(slot_block, home, states):
    blocks, width = home.shape[0], home.shape[2]
    outs = [jax.ShapeDtypeStruct(x.shape, x.dtype) for x in states]
    outs.append(jax.ShapeDtypeStruct((blocks, 4, width), jnp.bfloat16))
    return local_call(finish_kernel, "new_state", outs, [SCALARS] + [WHOLE] * 5)(
        slot_block, home, *states
    )


def on_core(zero, one):
    core = lax.axis_index("fsdp")
    pl.when(core == 0)(zero)
    pl.when(core != 0)(one)


def half_rows(left_t, right, moment):
    upper = moment.astype(jnp.bfloat16).astype(jnp.float32)
    rows = [right.astype(jnp.float32), left_t.astype(jnp.float32), upper, moment - upper]
    return jnp.concatenate(rows, axis=0)


def give_kernel(left_t, right, first, second, out, left_here, right_here, moment, done):
    copies = [
        pltpu.make_async_copy(left_t, left_here, done.at[0]),
        pltpu.make_async_copy(right, right_here, done.at[1]),
    ]
    first_copy = pltpu.make_async_copy(first, moment, done.at[2])
    second_copy = pltpu.make_async_copy(second, moment, done.at[2])
    on_core(second_copy.start, first_copy.start)
    for copy in copies:
        copy.start()
    for copy in copies:
        copy.wait()
    on_core(second_copy.wait, first_copy.wait)
    for slot in range(out.shape[0]):
        rows = half_rows(left_here[slot], right_here[slot], moment[slot])
        out[slot] = rows.astype(jnp.bfloat16)


def give_half(*states):
    blocks, rows, width = states[0].shape
    return local_call(
        give_kernel,
        "state_half",
        jax.ShapeDtypeStruct((blocks, 4 * rows, width), jnp.bfloat16),
        [FAR] * 4,
        [pltpu.VMEM(x.shape, x.dtype) for x in states[:3]] + [pltpu.SemaphoreType.DMA((3,))],
        vmem=60,
    )(*states)


def pack_kernel(slot_block, terms, given, left_t, right, first, second, out, *scratch):
    built, brought, left_here, right_here, moment, done, sent = scratch
    core = lax.axis_index("fsdp")
    blocks, span = terms.shape[0], terms.shape[2]
    units = pl.ds(0, span)
    fetch = [
        pltpu.make_async_copy(given, brought, done.at[blocks]),
        pltpu.make_async_copy(left_t, left_here, done.at[blocks + 1]),
        pltpu.make_async_copy(right, right_here, done.at[blocks + 2]),
    ]
    first_copy = pltpu.make_async_copy(first, moment, done.at[blocks + 3])
    second_copy = pltpu.make_async_copy(second, moment, done.at[blocks + 3])
    for copy in fetch:
        copy.start()
    on_core(first_copy.start, second_copy.start)
    near = [
        pltpu.make_async_copy(terms.at[b], built.at[b, :, units], done.at[b])
        for b in range(blocks)
    ]
    cross = [
        pltpu.make_async_copy(terms.at[b], built.at[:, b, units], done.at[b])
        for b in range(blocks)
    ]
    near_out = [pltpu.make_async_copy(built.at[b], out.at[b], sent.at[b]) for b in range(blocks)]
    cross_out = [
        pltpu.make_async_copy(built.at[:, b], out.at[:, b], sent.at[b]) for b in range(blocks)
    ]
    for b in range(blocks):
        on_core(near[b].start, cross[b].start)

    mine = slot_block[core, 0] >= 0
    n, col = iota((32, 32), 0), iota((32, 32), 1)
    turn = one_hot(col == (((n & 3) + 1) & 3) * 8 + (n >> 2))
    for copy in fetch:
        copy.wait()
    on_core(first_copy.wait, second_copy.wait)
    for b in range(blocks):
        at = 0
        for owner in range(slot_block.shape[0]):
            for slot in range(blocks):
                at += jnp.where(slot_block[owner, slot] == b, slot, 0)
        rows = half_rows(left_here[at], right_here[at], moment[at])
        rows = jnp.where(mine, rows, brought[at].astype(jnp.float32))
        half = jnp.where(core == 0, rows[:4], rows[4:8]).astype(jnp.bfloat16)
        singles = dot(turn, rows.astype(jnp.bfloat16)).astype(jnp.bfloat16)
        for g in EIGHT:
            to, then = jnp.where(core == 0, b, g), jnp.where(core == 0, g, b)
            built[to, then, span] = half
            built[to, then, span + 1] = singles[4 * g : 4 * g + 4]
        on_core(near[b].wait, cross[b].wait)
        on_core(near_out[b].start, cross_out[b].start)
    for b in range(blocks):
        on_core(near_out[b].wait, cross_out[b].wait)


def pack(slot_block, terms, given, *states):
    blocks, chips, span, rows, width = terms.shape
    out = jax.ShapeDtypeStruct((blocks, chips, span + 2, rows, width), terms.dtype)
    held = [pltpu.VMEM(x.shape, x.dtype) for x in (out, given, *states[:3])]
    return local_call(
        pack_kernel,
        "pack_messages",
        out,
        [SCALARS] + [FAR] * 6,
        held + [pltpu.SemaphoreType.DMA((blocks + 4,)), pltpu.SemaphoreType.DMA((blocks,))],
        vmem=60,
        out=FAR,
    )(slot_block, terms, given, *states)


def total_of(received, *at):
    return jnp.sum(received[(slice(None), *at)].astype(jnp.float32), axis=0)


def relay_kernel(received, out):
    span = received.shape[2] - 2
    for then in EIGHT:
        for unit in range(span):
            out[then, unit] = total_of(received, then, unit).astype(jnp.bfloat16)
        for source in EIGHT:
            at = span + 2 * source
            out[then, at] = received[source, then, span]
            out[then, at + 1] = received[source, then, span + 1]


def relay(received):
    span = received.shape[2] - 2
    shape = (GROUP, span + 2 * GROUP) + received.shape[3:]
    out = jax.ShapeDtypeStruct(shape, received.dtype)
    return local_call(relay_kernel, "relay", out, [WHOLE])(received)


def sum_kernel(received, copies, state):
    core = lax.axis_index("fsdp")
    span = received.shape[1] - 2 * GROUP
    total = jnp.concatenate([total_of(received, unit) for unit in range(span)], axis=0)
    total = total.astype(jnp.bfloat16)
    for peer in range(copies.shape[0]):
        copies[peer] = total
    for later in EIGHT:
        for early in EIGHT:
            one, two = PLACE[early, later], PLACE[later, early]
            to = jnp.where(core == 0, one, two)
            at = span + 2 * early
            state[to, 0] = received[later, at]
            state[to, 1] = received[later, at + 1]


def sum_terms(received):
    rows, width = received.shape[2:]
    span = received.shape[1] - 2 * GROUP
    outs = [
        jax.ShapeDtypeStruct((GROUP, span * rows, width), received.dtype),
        jax.ShapeDtypeStruct((GROUP * GROUP, 2, rows, width), received.dtype),
    ]
    return local_call(sum_kernel, "sum_terms", outs, [WHOLE])(received)


def shards(
    grad_parts,
    slot_block,
    gram_left,
    gram_right,
    left_basis_t,
    right_basis,
    moment_first,
    moment_second,
):
    blocks = grad_parts.shape[1]
    q_total = grad_parts.shape[2]
    half_span = grad_parts.shape[3]
    width = grad_parts.shape[4]
    core = lax.axis_index("fsdp")

    states = (left_basis_t, right_basis, moment_first, moment_second)
    terms = grad_parts[0].reshape(blocks, GROUP, q_total // GROUP, half_span, width)
    message = pack(slot_block, terms, swap_cores(give_half(*states)), *states)
    received = exchange(relay(exchange(message, FIRST)), SECOND)
    raw, half = sum_terms(received)
    raw = exchange(raw, BLOCK).reshape(-1, width)

    given = swap_cores(half)
    low = jnp.where(core == 0, half, given)
    high = jnp.where(core == 0, given, half)
    right = jnp.concatenate([low[:, 0], high[:, 0]], axis=1).reshape(width, width)
    left_t = low[:, 1, 0]
    first = low[:, 1, 1].astype(jnp.float32) + low[:, 1, 2].astype(jnp.float32)
    second = high[:, 1, 1].astype(jnp.float32) + high[:, 1, 2].astype(jnp.float32)

    home = chain(raw, swap_cores(raw), right, left_t, first, second)
    home = exchange(home.reshape(blocks * GROUP, 8, width), ALL)

    outs = finish(
        slot_block,
        home.reshape(blocks, GROUP * 8, width),
        (gram_left, gram_right, moment_first, moment_second),
    )
    return (*outs[:4], outs[4][:, None])


def solution(mesh):
    state = P("fsdp", "dp", None)
    return jax.shard_map(
        shards,
        mesh=mesh,
        in_specs=(P("dp", None, None, "fsdp", None), P()) + (state,) * 6,
        out_specs=(state,) * 4 + (P(None, "dp", "fsdp", None),),
        check_vma=False,
    )
```

```python
import jax
import jax.numpy as jnp
from jax import lax
from jax.experimental import pallas as pl
from jax.experimental.pallas import tpu as pltpu
from jax.sharding import PartitionSpec as P

shampoo_beta = 0.9
adam_first = 0.95
adam_second = 0.95
epsilon = 1e-08

GROUP = 8
AXES = ("fsdp", "dp")


def number(dp):
    b = g = 0
    for axis in range(3):
        place = (dp >> (2 * axis)) & 3
        wrap, inner = place >> 1, (place ^ (place >> 1)) & 1
        b += (inner if axis == 0 else wrap) << axis
        g += (wrap if axis == 0 else inner) << axis
    return b, g


PLACE = {number(dp): dp for dp in range(GROUP * GROUP)}
EIGHT = range(GROUP)


def device(c, b, g):
    return c * GROUP * GROUP + PLACE[b, g]


OVER_B = [[[device(c, b, g) for b in EIGHT] for g in EIGHT] for c in range(2)]
OVER_G = [[[device(c, b, g) for g in EIGHT] for b in EIGHT] for c in range(2)]
FIRST = OVER_B[0] + OVER_G[1]
SECOND = OVER_G[0] + OVER_B[1]
BLOCK = OVER_G[0] + OVER_G[1]
ALL = [[device(c, b, g) for b in EIGHT for g in EIGHT] for c in range(2)]


def exchange(x, groups):
    return lax.all_to_all(x, AXES, 0, 0, axis_index_groups=groups, tiled=True)


def swap_cores(x):
    return lax.ppermute(x, "fsdp", [(0, 1), (1, 0)])


def dot(a, b, ca=1, cb=0):
    return lax.dot_general(a, b, (((ca,), (cb,)), ((), ())), preferred_element_type=jnp.float32)


def iota(shape, axis):
    return lax.broadcasted_iota(jnp.int32, shape, axis)


def one_hot(hit):
    return jnp.where(hit, 1.0, 0.0).astype(jnp.bfloat16)


WHOLE = pl.BlockSpec(memory_space=pltpu.VMEM)
SCALARS = pl.BlockSpec(memory_space=pltpu.SMEM)
FAR = pl.BlockSpec(memory_space=pltpu.HBM)


def in_hbm(x):
    return pltpu.with_memory_space_constraint(x, pltpu.HBM)


def local_call(kernel, name, out_shape, in_specs, scratch=(), **options):
    return pl.pallas_call(
        kernel,
        out_shape=out_shape,
        in_specs=in_specs,
        out_specs=jax.tree.map(lambda _: WHOLE, out_shape),
        scratch_shapes=list(scratch),
        compiler_params=pltpu.CompilerParams(vmem_limit_bytes=40 * 2**20),
        name=name,
        **options,
    )


def chain_kernel(raw, swapped, right, left_t, first, second, out):
    bf16 = jnp.bfloat16
    core = lax.axis_index("fsdp")
    lane = number(lax.axis_index("dp"))[1]
    size = raw.shape[1]
    picks = size // 8

    n = iota((256, 256), 0)
    at = ((n >> 2) & 1) * 128 + (n >> 6) * 32 + ((n >> 3) & 7) * 4 + (n & 3)
    pick = one_hot(iota((256, 256), 1) == at)
    low = jnp.where(core == 0, raw[...], swapped[...])
    high = jnp.where(core == 0, swapped[...], raw[...])
    block = []
    for i in range(0, size // 2, 128):
        rows = jnp.concatenate([low[i : i + 128], high[i : i + 128]], axis=0)
        block.append(dot(pick, rows).astype(bf16))
    block = jnp.concatenate(block, axis=0)

    half_rot = dot(left_t[...], block).astype(bf16)
    rotated = dot(half_rot, right[...])
    new_first = adam_first * first[...] + (1.0 - adam_first) * rotated
    new_second = adam_second * second[...] + (1.0 - adam_second) * rotated * rotated
    scaled = (new_first / (jnp.sqrt(new_second) + epsilon)).astype(bf16)
    back = dot(scaled, right[...], 1, 1).astype(bf16)
    update = dot(left_t[...], back, 0, 0)

    own = one_hot(iota((picks, size), 1) == iota((picks, size), 0) * 8 + lane)
    gram_l = dot(dot(own, block).astype(bf16), block, 1, 1).astype(bf16)
    gram_r = dot(dot(block, own, 1, 1).astype(bf16), block, 0, 0).astype(bf16)

    upper = rotated.astype(bf16)
    lower = (rotated - upper.astype(jnp.float32)).astype(bf16)
    rows = jnp.concatenate([gram_l, gram_r, upper, lower], axis=0)
    n, col = iota((size, 4 * picks), 0), iota((size, 4 * picks), 1)
    spread = one_hot(col == ((n & 7) - 4 * (1 - core)) * picks + (n >> 3))
    kept = (iota((size, size), 0) & 4) == 4 * core
    result = jnp.where(kept, update, dot(spread, rows))
    order = [PLACE[b, g] * 8 for b in EIGHT for g in EIGHT]
    out[...] = jnp.concatenate([result[at : at + 8] for at in order], axis=0).astype(bf16)


def chain(raw, *others):
    width = raw.shape[1]
    out = jax.ShapeDtypeStruct((width, width), jnp.bfloat16)
    return local_call(chain_kernel, "block_chain", out, [WHOLE] * 6)(raw, *others)


def finish_kernel(slot_block, home, gram_l, gram_r, first, second, *outs):
    gram_l_new, gram_r_new, first_new, second_new, direction = outs
    core = lax.axis_index("fsdp")
    n, col = iota((32, 64), 0), iota((32, 64), 1)
    kind, chip, row = n >> 3, col >> 3, col & 7
    other = row - 4 * (1 - core)
    product = (chip == (n & 7)) & ((other == kind) | ((kind == 2) & (other == 3)))
    hit = ((kind == 3) & (row - 4 * core == (n & 7))) | ((kind < 3) & product)
    take = one_hot(hit)
    for b in range(home.shape[0]):
        direction[b] = dot(take[24:], home[b])[:4].astype(jnp.bfloat16)
    share = jnp.where(slot_block[core, 0] >= 0, 1.0, 0.0)
    for slot in range(home.shape[0]):
        block = jnp.maximum(slot_block[core, slot], 0)
        rows = dot(take, home[block]) * share
        rotated = rows[16:24]
        gram_l_new[slot] = shampoo_beta * gram_l[slot] + (1.0 - shampoo_beta) * rows[:8]
        gram_r_new[slot] = shampoo_beta * gram_r[slot] + (1.0 - shampoo_beta) * rows[8:16]
        first_new[slot] = adam_first * first[slot] + (1.0 - adam_first) * rotated
        second_new[slot] = (
            adam_second * second[slot] + (1.0 - adam_second) * rotated * rotated
        )


def finish(slot_block, home, states):
    blocks, width = home.shape[0], home.shape[2]
    outs = [jax.ShapeDtypeStruct(x.shape, x.dtype) for x in states]
    outs.append(jax.ShapeDtypeStruct((blocks, 4, width), jnp.bfloat16))
    return local_call(finish_kernel, "new_state", outs, [SCALARS] + [WHOLE] * 5)(
        slot_block, home, *states
    )


def on_core(zero, one):
    core = lax.axis_index("fsdp")
    pl.when(core == 0)(zero)
    pl.when(core != 0)(one)


def half_rows(left_t, right, moment):
    upper = moment.astype(jnp.bfloat16).astype(jnp.float32)
    rows = [right.astype(jnp.float32), left_t.astype(jnp.float32), upper, moment - upper]
    return jnp.concatenate(rows, axis=0)


def give_kernel(left_t, right, first, second, out, left_here, right_here, moment, done):
    copies = [
        pltpu.make_async_copy(left_t, left_here, done.at[0]),
        pltpu.make_async_copy(right, right_here, done.at[1]),
    ]
    first_copy = pltpu.make_async_copy(first, moment, done.at[2])
    second_copy = pltpu.make_async_copy(second, moment, done.at[2])
    on_core(second_copy.start, first_copy.start)
    for copy in copies:
        copy.start()
    for copy in copies:
        copy.wait()
    on_core(second_copy.wait, first_copy.wait)
    for slot in range(out.shape[0]):
        rows = half_rows(left_here[slot], right_here[slot], moment[slot])
        out[slot] = rows.astype(jnp.bfloat16)


def give_half(*states):
    blocks, rows, width = states[0].shape
    return local_call(
        give_kernel,
        "state_half",
        jax.ShapeDtypeStruct((blocks, 4 * rows, width), jnp.bfloat16),
        [FAR] * 4,
        [pltpu.VMEM(x.shape, x.dtype) for x in states[:3]] + [pltpu.SemaphoreType.DMA((3,))],
    )(*states)


def load_kernel(terms, out, done):
    blocks, units = terms.shape[0], pl.ds(0, terms.shape[2])
    near = [
        pltpu.make_async_copy(terms.at[b], out.at[b, :, units], done.at[b]) for b in range(blocks)
    ]
    cross = [
        pltpu.make_async_copy(terms.at[b], out.at[:, b, units], done.at[b]) for b in range(blocks)
    ]
    for b in range(blocks):
        on_core(near[b].start, cross[b].start)
    for b in range(blocks):
        on_core(near[b].wait, cross[b].wait)


def load(terms):
    blocks, chips, span, rows, width = terms.shape
    return local_call(
        load_kernel,
        "load_terms",
        jax.ShapeDtypeStruct((blocks, chips, span + 2, rows, width), terms.dtype),
        [FAR],
        [pltpu.SemaphoreType.DMA((blocks,))],
        cost_estimate=pl.CostEstimate(flops=0, bytes_accessed=2 * terms.nbytes, transcendentals=0),
    )(terms)


def pack_kernel(slot_block, loaded, given, left_t, right, first, second, out, *scratch):
    left_here, right_here, moment, done = scratch
    core = lax.axis_index("fsdp")
    blocks, span = out.shape[0], out.shape[2] - 2
    fetch = [
        pltpu.make_async_copy(left_t, left_here, done.at[0]),
        pltpu.make_async_copy(right, right_here, done.at[1]),
    ]
    first_copy = pltpu.make_async_copy(first, moment, done.at[2])
    second_copy = pltpu.make_async_copy(second, moment, done.at[2])
    for copy in fetch:
        copy.start()
    on_core(first_copy.start, second_copy.start)
    mine = slot_block[core, 0] >= 0
    n, col = iota((32, 32), 0), iota((32, 32), 1)
    turn = one_hot(col == (((n & 3) + 1) & 3) * 8 + (n >> 2))
    for copy in fetch:
        copy.wait()
    on_core(first_copy.wait, second_copy.wait)
    for b in range(blocks):
        at = 0
        for owner in range(slot_block.shape[0]):
            for slot in range(blocks):
                at += jnp.where(slot_block[owner, slot] == b, slot, 0)
        rows = half_rows(left_here[at], right_here[at], moment[at])
        rows = jnp.where(mine, rows, given[at].astype(jnp.float32))
        half = jnp.where(core == 0, rows[:4], rows[4:8]).astype(jnp.bfloat16)
        singles = dot(turn, rows.astype(jnp.bfloat16)).astype(jnp.bfloat16)
        for g in EIGHT:
            to, then = jnp.where(core == 0, b, g), jnp.where(core == 0, g, b)
            out[to, then, span] = half
            out[to, then, span + 1] = singles[4 * g : 4 * g + 4]


def pack(slot_block, loaded, given, *states):
    return local_call(
        pack_kernel,
        "pack_states",
        jax.ShapeDtypeStruct(loaded.shape, loaded.dtype),
        [SCALARS, WHOLE, WHOLE] + [FAR] * 4,
        [pltpu.VMEM(x.shape, x.dtype) for x in states[:3]] + [pltpu.SemaphoreType.DMA((3,))],
        input_output_aliases={1: 0},
    )(slot_block, loaded, given, *states)


def total_of(received, *at):
    return jnp.sum(received[(slice(None), *at)].astype(jnp.float32), axis=0)


def relay_kernel(received, out):
    span = received.shape[2] - 2
    for then in EIGHT:
        for unit in range(span):
            out[then, unit] = total_of(received, then, unit).astype(jnp.bfloat16)
        for source in EIGHT:
            at = span + 2 * source
            out[then, at] = received[source, then, span]
            out[then, at + 1] = received[source, then, span + 1]


def relay(received):
    span = received.shape[2] - 2
    shape = (GROUP, span + 2 * GROUP) + received.shape[3:]
    out = jax.ShapeDtypeStruct(shape, received.dtype)
    return local_call(relay_kernel, "relay", out, [WHOLE])(received)


def sum_kernel(received, copies, state):
    core = lax.axis_index("fsdp")
    span = received.shape[1] - 2 * GROUP
    total = jnp.concatenate([total_of(received, unit) for unit in range(span)], axis=0)
    total = total.astype(jnp.bfloat16)
    for peer in range(copies.shape[0]):
        copies[peer] = total
    for later in EIGHT:
        for early in EIGHT:
            one, two = PLACE[early, later], PLACE[later, early]
            to = jnp.where(core == 0, one, two)
            at = span + 2 * early
            state[to, 0] = received[later, at]
            state[to, 1] = received[later, at + 1]


def sum_terms(received):
    rows, width = received.shape[2:]
    span = received.shape[1] - 2 * GROUP
    outs = [
        jax.ShapeDtypeStruct((GROUP, span * rows, width), received.dtype),
        jax.ShapeDtypeStruct((GROUP * GROUP, 2, rows, width), received.dtype),
    ]
    return local_call(sum_kernel, "sum_terms", outs, [WHOLE])(received)


def shards(
    grad_parts,
    slot_block,
    gram_left,
    gram_right,
    left_basis_t,
    right_basis,
    moment_first,
    moment_second,
):
    blocks = grad_parts.shape[1]
    q_total = grad_parts.shape[2]
    half_span = grad_parts.shape[3]
    width = grad_parts.shape[4]
    core = lax.axis_index("fsdp")

    states = (left_basis_t, right_basis, moment_first, moment_second)
    states = tuple(in_hbm(part) for part in states)
    terms = grad_parts[0].reshape(blocks, GROUP, q_total // GROUP, half_span, width)
    terms = in_hbm(terms)
    message = pack(in_hbm(slot_block), load(terms), swap_cores(give_half(*states)), *states)
    received = exchange(relay(exchange(message, FIRST)), SECOND)
    raw, half = sum_terms(received)
    raw = exchange(raw, BLOCK).reshape(-1, width)

    given = swap_cores(half)
    low = jnp.where(core == 0, half, given)
    high = jnp.where(core == 0, given, half)
    right = jnp.concatenate([low[:, 0], high[:, 0]], axis=1).reshape(width, width)
    left_t = low[:, 1, 0]
    first = low[:, 1, 1].astype(jnp.float32) + low[:, 1, 2].astype(jnp.float32)
    second = high[:, 1, 1].astype(jnp.float32) + high[:, 1, 2].astype(jnp.float32)

    home = chain(raw, swap_cores(raw), right, left_t, first, second)
    home = exchange(home.reshape(blocks * GROUP, 8, width), ALL)

    outs = finish(
        slot_block,
        home.reshape(blocks, GROUP * 8, width),
        (gram_left, gram_right, moment_first, moment_second),
    )
    return (*outs[:4], outs[4][:, None])


def solution(mesh):
    state = P("fsdp", "dp", None)
    return jax.shard_map(
        shards,
        mesh=mesh,
        in_specs=(P("dp", None, None, "fsdp", None), P()) + (state,) * 6,
        out_specs=(state,) * 4 + (P(None, "dp", "fsdp", None),),
        check_vma=False,
    )
```

```python
import jax
import jax.numpy as jnp
from jax import lax
from jax.experimental import pallas as pl
from jax.experimental.pallas import tpu as pltpu
from jax.sharding import PartitionSpec as P

shampoo_beta = 0.9
adam_first = 0.95
adam_second = 0.95
epsilon = 1e-08

GROUP = 8
AXES = ("fsdp", "dp")


def number(dp):
    b = g = 0
    for axis in range(3):
        place = (dp >> (2 * axis)) & 3
        wrap, inner = place >> 1, (place ^ (place >> 1)) & 1
        b += (inner if axis == 2 else wrap) << axis
        g += (wrap if axis == 2 else inner) << axis
    return b, g


PLACE = {number(dp): dp for dp in range(GROUP * GROUP)}
EIGHT = range(GROUP)


def device(c, b, g):
    return c * GROUP * GROUP + PLACE[b, g]


OVER_B = [[[device(c, b, g) for b in EIGHT] for g in EIGHT] for c in range(2)]
OVER_G = [[[device(c, b, g) for g in EIGHT] for b in EIGHT] for c in range(2)]
FIRST = OVER_B[0] + OVER_G[1]
SECOND = OVER_G[0] + OVER_B[1]
BLOCK = OVER_G[0] + OVER_G[1]
ALL = [[device(c, b, g) for b in EIGHT for g in EIGHT] for c in range(2)]


def exchange(x, groups):
    return lax.all_to_all(x, AXES, 0, 0, axis_index_groups=groups, tiled=True)


def swap_cores(x):
    return lax.ppermute(x, "fsdp", [(0, 1), (1, 0)])


def dot(a, b, ca=1, cb=0):
    return lax.dot_general(a, b, (((ca,), (cb,)), ((), ())), preferred_element_type=jnp.float32)


def iota(shape, axis):
    return lax.broadcasted_iota(jnp.int32, shape, axis)


def one_hot(hit):
    return jnp.where(hit, 1.0, 0.0).astype(jnp.bfloat16)


WHOLE = pl.BlockSpec(memory_space=pltpu.VMEM)
SCALARS = pl.BlockSpec(memory_space=pltpu.SMEM)
FAR = pl.BlockSpec(memory_space=pltpu.HBM)


def in_hbm(x):
    return pltpu.with_memory_space_constraint(x, pltpu.HBM)


def local_call(kernel, name, out_shape, in_specs, scratch=(), out=WHOLE, **options):
    return pl.pallas_call(
        kernel,
        out_shape=out_shape,
        in_specs=in_specs,
        out_specs=jax.tree.map(lambda _: out, out_shape),
        scratch_shapes=list(scratch),
        compiler_params=pltpu.CompilerParams(vmem_limit_bytes=40 * 2**20),
        name=name,
        **options,
    )


def chain_kernel(raw, swapped, right, left_t, first, second, out):
    bf16 = jnp.bfloat16
    core = lax.axis_index("fsdp")
    lane = number(lax.axis_index("dp"))[1]
    size = raw.shape[1]
    picks = size // 8

    n = iota((256, 256), 0)
    at = ((n >> 2) & 1) * 128 + (n >> 6) * 32 + ((n >> 3) & 7) * 4 + (n & 3)
    pick = one_hot(iota((256, 256), 1) == at)
    low = jnp.where(core == 0, raw[...], swapped[...])
    high = jnp.where(core == 0, swapped[...], raw[...])
    block = []
    for i in range(0, size // 2, 128):
        rows = jnp.concatenate([low[i : i + 128], high[i : i + 128]], axis=0)
        block.append(dot(pick, rows).astype(bf16))
    block = jnp.concatenate(block, axis=0)

    half_rot = dot(left_t[...], block).astype(bf16)
    rotated = dot(half_rot, right[...])
    new_first = adam_first * first[...] + (1.0 - adam_first) * rotated
    new_second = adam_second * second[...] + (1.0 - adam_second) * rotated * rotated
    scaled = (new_first / (jnp.sqrt(new_second) + epsilon)).astype(bf16)
    back = dot(scaled, right[...], 1, 1).astype(bf16)
    update = dot(left_t[...], back, 0, 0)

    own = one_hot(iota((picks, size), 1) == iota((picks, size), 0) * 8 + lane)
    gram_l = dot(dot(own, block).astype(bf16), block, 1, 1).astype(bf16)
    gram_r = dot(dot(block, own, 1, 1).astype(bf16), block, 0, 0).astype(bf16)

    upper = rotated.astype(bf16)
    lower = (rotated - upper.astype(jnp.float32)).astype(bf16)
    rows = jnp.concatenate([gram_l, gram_r, upper, lower], axis=0)
    n, col = iota((size, 4 * picks), 0), iota((size, 4 * picks), 1)
    spread = one_hot(col == ((n & 7) - 4 * (1 - core)) * picks + (n >> 3))
    kept = (iota((size, size), 0) & 4) == 4 * core
    result = jnp.where(kept, update, dot(spread, rows))
    order = [PLACE[b, g] * 8 for b in EIGHT for g in EIGHT]
    out[...] = jnp.concatenate([result[at : at + 8] for at in order], axis=0).astype(bf16)


def chain(raw, *others):
    width = raw.shape[1]
    out = jax.ShapeDtypeStruct((width, width), jnp.bfloat16)
    return local_call(chain_kernel, "block_chain", out, [WHOLE] * 6)(raw, *others)


def finish_kernel(slot_block, home, gram_l, gram_r, first, second, *refs):
    outs, built, sent = refs[:5], refs[5:10], refs[10]
    core = lax.axis_index("fsdp")
    blocks = home.shape[0]
    n, col = iota((32, 64), 0), iota((32, 64), 1)
    kind, chip, row = n >> 3, col >> 3, col & 7
    other = row - 4 * (1 - core)
    product = (chip == (n & 7)) & ((other == kind) | ((kind == 2) & (other == 3)))
    hit = ((kind == 3) & (row - 4 * core == (n & 7))) | ((kind < 3) & product)
    take = one_hot(hit)
    share = jnp.where(slot_block[core, 0] >= 0, 1.0, 0.0)
    copies = []
    for slot in range(blocks):
        block = jnp.maximum(slot_block[core, slot], 0)
        rows = dot(take, home[block]) * share
        rotated = rows[16:24]
        built[0][slot] = shampoo_beta * gram_l[slot] + (1.0 - shampoo_beta) * rows[:8]
        built[1][slot] = shampoo_beta * gram_r[slot] + (1.0 - shampoo_beta) * rows[8:16]
        built[2][slot] = adam_first * first[slot] + (1.0 - adam_first) * rotated
        built[3][slot] = (
            adam_second * second[slot] + (1.0 - adam_second) * rotated * rotated
        )
        if slot % 4 == 3:
            part = pl.ds(slot - 3, 4)
            for i in range(4):
                copies.append(
                    pltpu.make_async_copy(
                        built[i].at[part], outs[i].at[part], sent.at[i, slot // 4]
                    )
                )
                copies[-1].start()
    for b in range(blocks):
        built[4][b] = dot(take[24:], home[b])[:4].astype(jnp.bfloat16)
    copies.append(pltpu.make_async_copy(built[4], outs[4], sent.at[4, 0]))
    copies[-1].start()
    for copy in copies:
        copy.wait()


def finish(slot_block, home, states):
    blocks, width = home.shape[0], home.shape[2]
    outs = [jax.ShapeDtypeStruct(x.shape, x.dtype) for x in states]
    outs.append(jax.ShapeDtypeStruct((blocks, 4, width), jnp.bfloat16))
    return local_call(
        finish_kernel,
        "new_state",
        outs,
        [SCALARS] + [WHOLE] * 5,
        [pltpu.VMEM(x.shape, x.dtype) for x in outs] + [pltpu.SemaphoreType.DMA((5, 2))],
        out=FAR,
    )(slot_block, home, *states)


def on_core(zero, one):
    core = lax.axis_index("fsdp")
    pl.when(core == 0)(zero)
    pl.when(core != 0)(one)


def half_rows(left_t, right, moment):
    upper = moment.astype(jnp.bfloat16).astype(jnp.float32)
    rows = [right.astype(jnp.float32), left_t.astype(jnp.float32), upper, moment - upper]
    return jnp.concatenate(rows, axis=0)


def halves_kernel(left_t, right, first, second, keep, give, *scratch):
    held, done = scratch[:4], scratch[4]
    copies = [
        pltpu.make_async_copy(source, to, done.at[i])
        for i, (source, to) in enumerate(zip((left_t, right, first, second), held))
    ]
    for copy in copies:
        copy.start()
    for copy in copies:
        copy.wait()
    core = lax.axis_index("fsdp")
    for slot in range(keep.shape[0]):
        left_rows, right_rows, one, two = (part[slot] for part in held)
        for out, moment in (
            (keep, jnp.where(core == 0, one, two)),
            (give, jnp.where(core == 0, two, one)),
        ):
            out[slot] = half_rows(left_rows, right_rows, moment).astype(jnp.bfloat16)


def halves(*states):
    blocks, rows, width = states[0].shape
    return local_call(
        halves_kernel,
        "state_halves",
        [jax.ShapeDtypeStruct((blocks, 4 * rows, width), jnp.bfloat16)] * 2,
        [FAR] * 4,
        [pltpu.VMEM(x.shape, x.dtype) for x in states] + [pltpu.SemaphoreType.DMA((4,))],
    )(*states)


def load_kernel(terms, out, done):
    blocks, units = terms.shape[0], pl.ds(0, terms.shape[2])
    near = [
        pltpu.make_async_copy(terms.at[b], out.at[b, :, units], done.at[b]) for b in range(blocks)
    ]
    cross = [
        pltpu.make_async_copy(terms.at[b], out.at[:, b, units], done.at[b]) for b in range(blocks)
    ]
    for b in range(blocks):
        on_core(near[b].start, cross[b].start)
    for b in range(blocks):
        on_core(near[b].wait, cross[b].wait)


def load(terms):
    blocks, chips, span, rows, width = terms.shape
    return local_call(
        load_kernel,
        "load_terms",
        jax.ShapeDtypeStruct((blocks, chips, span + 2, rows, width), terms.dtype),
        [FAR],
        [pltpu.SemaphoreType.DMA((blocks,))],
        cost_estimate=pl.CostEstimate(flops=0, bytes_accessed=2 * terms.nbytes, transcendentals=0),
    )(terms)


def pack_kernel(slot_block, loaded, keep, given, out):
    core = lax.axis_index("fsdp")
    blocks, span = out.shape[0], out.shape[2] - 2
    mine = slot_block[core, 0] >= 0
    n, col = iota((32, 32), 0), iota((32, 32), 1)
    turn = one_hot(col == (((n & 3) + 1) & 3) * 8 + (n >> 2))
    for b in range(blocks):
        at = 0
        for owner in range(slot_block.shape[0]):
            for slot in range(blocks):
                at += jnp.where(slot_block[owner, slot] == b, slot, 0)
        rows = jnp.where(mine, keep[at], given[at])
        half = rows[:8].astype(jnp.float32)
        half = jnp.where(core == 0, half[:4], half[4:]).astype(jnp.bfloat16)
        singles = dot(turn, rows).astype(jnp.bfloat16)
        for g in EIGHT:
            to, then = jnp.where(core == 0, b, g), jnp.where(core == 0, g, b)
            out[to, then, span] = half
            out[to, then, span + 1] = singles[4 * g : 4 * g + 4]


def pack(slot_block, loaded, keep, given):
    return local_call(
        pack_kernel,
        "pack_states",
        jax.ShapeDtypeStruct(loaded.shape, loaded.dtype),
        [SCALARS] + [WHOLE] * 3,
        input_output_aliases={1: 0},
    )(slot_block, loaded, keep, given)


def total_of(received, *at):
    return jnp.sum(received[(slice(None), *at)].astype(jnp.float32), axis=0)


def relay_kernel(received, out):
    span = received.shape[2] - 2
    for then in EIGHT:
        for unit in range(span):
            out[then, unit] = total_of(received, then, unit).astype(jnp.bfloat16)
        for source in EIGHT:
            at = span + 2 * source
            out[then, at] = received[source, then, span]
            out[then, at + 1] = received[source, then, span + 1]


def relay(received):
    span = received.shape[2] - 2
    shape = (GROUP, span + 2 * GROUP) + received.shape[3:]
    out = jax.ShapeDtypeStruct(shape, received.dtype)
    return local_call(relay_kernel, "relay", out, [WHOLE])(received)


def sum_kernel(received, copies, state):
    core = lax.axis_index("fsdp")
    span = received.shape[1] - 2 * GROUP
    total = jnp.concatenate([total_of(received, unit) for unit in range(span)], axis=0)
    total = total.astype(jnp.bfloat16)
    for peer in range(copies.shape[0]):
        copies[peer] = total
    for later in EIGHT:
        for early in EIGHT:
            one, two = PLACE[early, later], PLACE[later, early]
            to = jnp.where(core == 0, one, two)
            at = span + 2 * early
            state[to, 0] = received[later, at]
            state[to, 1] = received[later, at + 1]


def sum_terms(received):
    rows, width = received.shape[2:]
    span = received.shape[1] - 2 * GROUP
    outs = [
        jax.ShapeDtypeStruct((GROUP, span * rows, width), received.dtype),
        jax.ShapeDtypeStruct((GROUP * GROUP, 2, rows, width), received.dtype),
    ]
    return local_call(sum_kernel, "sum_terms", outs, [WHOLE])(received)


def shards(
    grad_parts,
    slot_block,
    gram_left,
    gram_right,
    left_basis_t,
    right_basis,
    moment_first,
    moment_second,
):
    blocks = grad_parts.shape[1]
    q_total = grad_parts.shape[2]
    half_span = grad_parts.shape[3]
    width = grad_parts.shape[4]
    core = lax.axis_index("fsdp")

    states = (left_basis_t, right_basis, moment_first, moment_second)
    states = tuple(in_hbm(part) for part in states)
    terms = grad_parts[0].reshape(blocks, GROUP, q_total // GROUP, half_span, width)
    terms = in_hbm(terms)
    keep, give = halves(*states)
    message = pack(in_hbm(slot_block), load(terms), keep, swap_cores(give))
    received = exchange(relay(exchange(message, FIRST)), SECOND)
    raw, half = sum_terms(received)
    raw = exchange(raw, BLOCK).reshape(-1, width)

    given = swap_cores(half)
    low = jnp.where(core == 0, half, given)
    high = jnp.where(core == 0, given, half)
    right = jnp.concatenate([low[:, 0], high[:, 0]], axis=1).reshape(width, width)
    left_t = low[:, 1, 0]
    first = low[:, 1, 1].astype(jnp.float32) + low[:, 1, 2].astype(jnp.float32)
    second = high[:, 1, 1].astype(jnp.float32) + high[:, 1, 2].astype(jnp.float32)

    home = chain(raw, swap_cores(raw), right, left_t, first, second)
    home = exchange(home.reshape(blocks * GROUP, 8, width), ALL)

    outs = finish(
        slot_block,
        home.reshape(blocks, GROUP * 8, width),
        (gram_left, gram_right, moment_first, moment_second),
    )
    return (*outs[:4], outs[4][:, None])


def solution(mesh):
    state = P("fsdp", "dp", None)
    return jax.shard_map(
        shards,
        mesh=mesh,
        in_specs=(P("dp", None, None, "fsdp", None), P()) + (state,) * 6,
        out_specs=(state,) * 4 + (P(None, "dp", "fsdp", None),),
        check_vma=False,
    )
```

```python
import jax
import jax.numpy as jnp
from jax import lax
from jax.experimental import pallas as pl
from jax.experimental.pallas import tpu as pltpu
from jax.sharding import PartitionSpec as P

shampoo_beta = 0.9
adam_first = 0.95
adam_second = 0.95
epsilon = 1e-08

GROUP = 8
AXES = ("fsdp", "dp")


def number(dp):
    b = g = 0
    for axis in range(3):
        place = (dp >> (2 * axis)) & 3
        wrap, inner = place >> 1, (place ^ (place >> 1)) & 1
        b += (inner if axis == 2 else wrap) << axis
        g += (wrap if axis == 2 else inner) << axis
    return b, g


PLACE = {number(dp): dp for dp in range(GROUP * GROUP)}
EIGHT = range(GROUP)


def device(c, b, g):
    return c * GROUP * GROUP + PLACE[b, g]


OVER_B = [[[device(c, b, g) for b in EIGHT] for g in EIGHT] for c in range(2)]
OVER_G = [[[device(c, b, g) for g in EIGHT] for b in EIGHT] for c in range(2)]
FIRST = OVER_B[0] + OVER_G[1]
SECOND = OVER_G[0] + OVER_B[1]
BLOCK = OVER_G[0] + OVER_G[1]
ALL = [[device(c, b, g) for b in EIGHT for g in EIGHT] for c in range(2)]


def exchange(x, groups):
    return lax.all_to_all(x, AXES, 0, 0, axis_index_groups=groups, tiled=True)


def swap_cores(x):
    return lax.ppermute(x, "fsdp", [(0, 1), (1, 0)])


def dot(a, b, ca=1, cb=0):
    return lax.dot_general(a, b, (((ca,), (cb,)), ((), ())), preferred_element_type=jnp.float32)


def iota(shape, axis):
    return lax.broadcasted_iota(jnp.int32, shape, axis)


def one_hot(hit):
    return jnp.where(hit, 1.0, 0.0).astype(jnp.bfloat16)


WHOLE = pl.BlockSpec(memory_space=pltpu.VMEM)
SCALARS = pl.BlockSpec(memory_space=pltpu.SMEM)
FAR = pl.BlockSpec(memory_space=pltpu.HBM)


def in_hbm(x):
    return pltpu.with_memory_space_constraint(x, pltpu.HBM)


def local_call(kernel, name, out_shape, in_specs, scratch=(), out=WHOLE, **options):
    return pl.pallas_call(
        kernel,
        out_shape=out_shape,
        in_specs=in_specs,
        out_specs=jax.tree.map(lambda _: out, out_shape),
        scratch_shapes=list(scratch),
        compiler_params=pltpu.CompilerParams(vmem_limit_bytes=40 * 2**20),
        name=name,
        **options,
    )


def chain_kernel(raw, swapped, right, left_t, first, second, out):
    bf16 = jnp.bfloat16
    core = lax.axis_index("fsdp")
    lane = number(lax.axis_index("dp"))[1]
    size = raw.shape[1]
    picks = size // 8

    n = iota((256, 256), 0)
    at = ((n >> 2) & 1) * 128 + (n >> 6) * 32 + ((n >> 3) & 7) * 4 + (n & 3)
    pick = one_hot(iota((256, 256), 1) == at)
    low = jnp.where(core == 0, raw[...], swapped[...])
    high = jnp.where(core == 0, swapped[...], raw[...])
    block = []
    for i in range(0, size // 2, 128):
        rows = jnp.concatenate([low[i : i + 128], high[i : i + 128]], axis=0)
        block.append(dot(pick, rows).astype(bf16))
    block = jnp.concatenate(block, axis=0)

    half_rot = dot(left_t[...], block).astype(bf16)
    rotated = dot(half_rot, right[...])
    new_first = adam_first * first[...] + (1.0 - adam_first) * rotated
    new_second = adam_second * second[...] + (1.0 - adam_second) * rotated * rotated
    scaled = (new_first / (jnp.sqrt(new_second) + epsilon)).astype(bf16)
    back = dot(scaled, right[...], 1, 1).astype(bf16)
    update = dot(left_t[...], back, 0, 0)

    own = one_hot(iota((picks, size), 1) == iota((picks, size), 0) * 8 + lane)
    gram_l = dot(dot(own, block).astype(bf16), block, 1, 1).astype(bf16)
    gram_r = dot(dot(block, own, 1, 1).astype(bf16), block, 0, 0).astype(bf16)

    upper = rotated.astype(bf16)
    lower = (rotated - upper.astype(jnp.float32)).astype(bf16)
    rows = jnp.concatenate([gram_l, gram_r, upper, lower], axis=0)
    n, col = iota((size, 4 * picks), 0), iota((size, 4 * picks), 1)
    spread = one_hot(col == ((n & 7) - 4 * (1 - core)) * picks + (n >> 3))
    kept = (iota((size, size), 0) & 4) == 4 * core
    result = jnp.where(kept, update, dot(spread, rows))
    order = [PLACE[b, g] * 8 for b in EIGHT for g in EIGHT]
    out[...] = jnp.concatenate([result[at : at + 8] for at in order], axis=0).astype(bf16)


def chain(raw, *others):
    width = raw.shape[1]
    out = jax.ShapeDtypeStruct((width, width), jnp.bfloat16)
    return local_call(chain_kernel, "block_chain", out, [WHOLE] * 6)(raw, *others)


def finish_kernel(slot_block, home, gram_l, gram_r, first, second, *refs):
    outs, built, sent = refs[:5], refs[5:10], refs[10]
    core = lax.axis_index("fsdp")
    blocks = home.shape[0]
    n, col = iota((32, 64), 0), iota((32, 64), 1)
    kind, chip, row = n >> 3, col >> 3, col & 7
    other = row - 4 * (1 - core)
    product = (chip == (n & 7)) & ((other == kind) | ((kind == 2) & (other == 3)))
    hit = ((kind == 3) & (row - 4 * core == (n & 7))) | ((kind < 3) & product)
    take = one_hot(hit)
    share = jnp.where(slot_block[core, 0] >= 0, 1.0, 0.0)
    copies = []
    for slot in range(blocks):
        block = jnp.maximum(slot_block[core, slot], 0)
        rows = dot(take, home[block]) * share
        rotated = rows[16:24]
        built[0][slot] = shampoo_beta * gram_l[slot] + (1.0 - shampoo_beta) * rows[:8]
        built[1][slot] = shampoo_beta * gram_r[slot] + (1.0 - shampoo_beta) * rows[8:16]
        built[2][slot] = adam_first * first[slot] + (1.0 - adam_first) * rotated
        built[3][slot] = (
            adam_second * second[slot] + (1.0 - adam_second) * rotated * rotated
        )
        if slot % 4 == 3:
            part = pl.ds(slot - 3, 4)
            for i in range(4):
                copies.append(
                    pltpu.make_async_copy(
                        built[i].at[part], outs[i].at[part], sent.at[i, slot // 4]
                    )
                )
                copies[-1].start()
    for b in range(blocks):
        built[4][b] = dot(take[24:], home[b])[:4].astype(jnp.bfloat16)
    copies.append(pltpu.make_async_copy(built[4], outs[4], sent.at[4, 0]))
    copies[-1].start()
    for copy in copies:
        copy.wait()


def finish(slot_block, home, states):
    blocks, width = home.shape[0], home.shape[2]
    outs = [jax.ShapeDtypeStruct(x.shape, x.dtype) for x in states]
    outs.append(jax.ShapeDtypeStruct((blocks, 4, width), jnp.bfloat16))
    return local_call(
        finish_kernel,
        "new_state",
        outs,
        [SCALARS] + [WHOLE] * 5,
        [pltpu.VMEM(x.shape, x.dtype) for x in outs] + [pltpu.SemaphoreType.DMA((5, 2))],
        out=FAR,
    )(slot_block, home, *states)


def on_core(zero, one):
    core = lax.axis_index("fsdp")
    pl.when(core == 0)(zero)
    pl.when(core != 0)(one)


def halves_kernel(left_t, right, first, second, keep, give, *scratch):
    held, done = scratch[:4], scratch[4]
    copies = [
        pltpu.make_async_copy(source, to, done.at[i])
        for i, (source, to) in enumerate(zip((left_t, right, first, second), held))
    ]
    for copy in copies:
        copy.start()
    for copy in copies:
        copy.wait()
    core = lax.axis_index("fsdp")
    for slot in range(keep.shape[0]):
        left_rows, right_rows, one, two = (part[slot].astype(jnp.float32) for part in held)
        upper = one.astype(jnp.bfloat16).astype(jnp.float32)
        whole = jnp.concatenate([right_rows] * 4, axis=0)
        singles = jnp.concatenate([left_rows, upper, one - upper, two], axis=0)
        keep[slot] = jnp.where(core == 0, whole, singles).astype(jnp.bfloat16)
        give[slot] = jnp.where(core == 0, singles, whole).astype(jnp.bfloat16)


def halves(*states):
    blocks, rows, width = states[0].shape
    return local_call(
        halves_kernel,
        "state_halves",
        [jax.ShapeDtypeStruct((blocks, 4 * rows, width), jnp.bfloat16)] * 2,
        [FAR] * 4,
        [pltpu.VMEM(x.shape, x.dtype) for x in states] + [pltpu.SemaphoreType.DMA((4,))],
    )(*states)


def load_kernel(terms, by_block, out, done):
    blocks, chips, span = terms.shape[:3]
    near = [
        pltpu.make_async_copy(by_block.at[b], out.at[b, pl.ds(0, chips * span)], done.at[b])
        for b in range(blocks)
    ]
    cross = [
        pltpu.make_async_copy(terms.at[b], out.at[:, pl.ds(b * span, span)], done.at[b])
        for b in range(blocks)
    ]
    for b in range(blocks):
        on_core(near[b].start, cross[b].start)
    for b in range(blocks):
        on_core(near[b].wait, cross[b].wait)


def load(terms):
    blocks, chips, span, rows, width = terms.shape
    return local_call(
        load_kernel,
        "load_terms",
        jax.ShapeDtypeStruct((blocks, chips * span + GROUP, rows, width), terms.dtype),
        [FAR] * 2,
        [pltpu.SemaphoreType.DMA((blocks,))],
        cost_estimate=pl.CostEstimate(flops=0, bytes_accessed=2 * terms.nbytes, transcendentals=0),
    )(in_hbm(terms), in_hbm(terms.reshape(blocks, chips * span, rows, width)))


def pack_kernel(slot_block, loaded, keep, given, out):
    core = lax.axis_index("fsdp")
    blocks = out.shape[0]
    units = out.shape[1] - GROUP
    mine = slot_block[core, 0] >= 0
    n, col = iota((32, 32), 0), iota((32, 32), 1)
    turn = one_hot(col == (n & 3) * 8 + (n >> 2))
    for b in range(blocks):
        at = 0
        for owner in range(slot_block.shape[0]):
            for slot in range(blocks):
                at += jnp.where(slot_block[owner, slot] == b, slot, 0)
        rows = jnp.where(mine, keep[at], given[at])

        def whole(b=b, rows=rows):
            right = rows[:8].astype(jnp.float32)
            out[b, units] = right[:4].astype(jnp.bfloat16)
            out[b, units + 1] = right[4:].astype(jnp.bfloat16)

        def singles(b=b, rows=rows):
            turned = dot(turn, rows).astype(jnp.bfloat16)
            for g in EIGHT:
                out[g, units + b] = turned[4 * g : 4 * g + 4]

        on_core(whole, singles)


def pack(slot_block, loaded, keep, given):
    return local_call(
        pack_kernel,
        "pack_states",
        jax.ShapeDtypeStruct(loaded.shape, loaded.dtype),
        [SCALARS] + [WHOLE] * 3,
        input_output_aliases={1: 0},
    )(slot_block, loaded, keep, given)


def total_of(received, *at):
    return jnp.sum(received[(slice(None), *at)].astype(jnp.float32), axis=0)


def relay_kernel(received, out):
    units = received.shape[1] - GROUP
    span = units // GROUP
    for then in EIGHT:
        for unit in range(span):
            total = total_of(received, then * span + unit)
            out[then, unit] = total.astype(jnp.bfloat16)

    def whole():
        for source in EIGHT:
            for i in range(2):
                rows = received[source, units + i]
                for then in EIGHT:
                    out[then, span + 2 * source + i] = rows

    def singles():
        for source in EIGHT:
            for then in EIGHT:
                out[then, span + source] = received[source, units + then]

    on_core(whole, singles)


def relay(received):
    span = received.shape[1] // GROUP - 1
    shape = (GROUP, span + 2 * GROUP) + received.shape[2:]
    out = jax.ShapeDtypeStruct(shape, received.dtype)
    return local_call(relay_kernel, "relay", out, [WHOLE])(received)


def sum_kernel(received, copies, state):
    span = received.shape[1] - 2 * GROUP
    total = jnp.concatenate([total_of(received, unit) for unit in range(span)], axis=0)
    total = total.astype(jnp.bfloat16)
    for peer in range(copies.shape[0]):
        copies[peer] = total

    def whole():
        for later in EIGHT:
            for early in EIGHT:
                for i in range(2):
                    state[PLACE[early, later], i] = received[later, span + 2 * early + i]

    def singles():
        for later in EIGHT:
            for early in EIGHT:
                state[PLACE[later, early], 0] = received[later, span + early]

    on_core(whole, singles)


def sum_terms(received):
    rows, width = received.shape[2:]
    span = received.shape[1] - 2 * GROUP
    outs = [
        jax.ShapeDtypeStruct((GROUP, span * rows, width), received.dtype),
        jax.ShapeDtypeStruct((GROUP * GROUP, 2, rows, width), received.dtype),
    ]
    return local_call(sum_kernel, "sum_terms", outs, [WHOLE])(received)


def shards(
    grad_parts,
    slot_block,
    gram_left,
    gram_right,
    left_basis_t,
    right_basis,
    moment_first,
    moment_second,
):
    blocks = grad_parts.shape[1]
    q_total = grad_parts.shape[2]
    half_span = grad_parts.shape[3]
    width = grad_parts.shape[4]
    core = lax.axis_index("fsdp")

    states = (left_basis_t, right_basis, moment_first, moment_second)
    states = tuple(in_hbm(part) for part in states)
    terms = grad_parts[0].reshape(blocks, GROUP, q_total // GROUP, half_span, width)
    keep, give = halves(*states)
    message = pack(in_hbm(slot_block), load(terms), keep, swap_cores(give))
    received = exchange(relay(exchange(message, FIRST)), SECOND)
    raw, half = sum_terms(received)
    raw = exchange(raw, BLOCK).reshape(-1, width)

    given = swap_cores(half)
    right = jnp.where(core == 0, half, given).reshape(width, width)
    singles = jnp.where(core == 0, given, half)[:, 0]
    left_t = singles[:, 0]
    first = singles[:, 1].astype(jnp.float32) + singles[:, 2].astype(jnp.float32)
    second = singles[:, 3].astype(jnp.float32)

    home = chain(raw, swap_cores(raw), right, left_t, first, second)
    home = exchange(home.reshape(blocks * GROUP, 8, width), ALL)

    outs = finish(
        slot_block,
        home.reshape(blocks, GROUP * 8, width),
        (gram_left, gram_right, moment_first, moment_second),
    )
    return (*outs[:4], outs[4][:, None])


def solution(mesh):
    state = P("fsdp", "dp", None)
    return jax.shard_map(
        shards,
        mesh=mesh,
        in_specs=(P("dp", None, None, "fsdp", None), P()) + (state,) * 6,
        out_specs=(state,) * 4 + (P(None, "dp", "fsdp", None),),
        check_vma=False,
    )
```

```python
import jax
import jax.numpy as jnp
from jax import lax
from jax.experimental import pallas as pl
from jax.experimental.pallas import tpu as pltpu
from jax.sharding import PartitionSpec as P

shampoo_beta = 0.9
adam_first = 0.95
adam_second = 0.95
epsilon = 1e-08

GROUP = 8
AXES = ("fsdp", "dp")


def number(dp):
    b = g = 0
    for axis in range(3):
        place = (dp >> (2 * axis)) & 3
        wrap, inner = place >> 1, (place ^ (place >> 1)) & 1
        b += (wrap if axis == 2 else inner) << axis
        g += (inner if axis == 2 else wrap) << axis
    return b, g


PLACE = {number(dp): dp for dp in range(GROUP * GROUP)}
EIGHT = range(GROUP)


def device(c, b, g):
    return c * GROUP * GROUP + PLACE[b, g]


OVER_B = [[[device(c, b, g) for b in EIGHT] for g in EIGHT] for c in range(2)]
OVER_G = [[[device(c, b, g) for g in EIGHT] for b in EIGHT] for c in range(2)]
FIRST = OVER_B[0] + OVER_G[1]
SECOND = OVER_G[0] + OVER_B[1]
BLOCK = OVER_G[0] + OVER_G[1]
ALL = [[device(c, b, g) for b in EIGHT for g in EIGHT] for c in range(2)]


def exchange(x, groups):
    return lax.all_to_all(x, AXES, 0, 0, axis_index_groups=groups, tiled=True)


def swap_cores(x):
    return lax.ppermute(x, "fsdp", [(0, 1), (1, 0)])


def dot(a, b, ca=1, cb=0):
    return lax.dot_general(a, b, (((ca,), (cb,)), ((), ())), preferred_element_type=jnp.float32)


def iota(shape, axis):
    return lax.broadcasted_iota(jnp.int32, shape, axis)


def one_hot(hit):
    return jnp.where(hit, 1.0, 0.0).astype(jnp.bfloat16)


WHOLE = pl.BlockSpec(memory_space=pltpu.VMEM)
SCALARS = pl.BlockSpec(memory_space=pltpu.SMEM)
FAR = pl.BlockSpec(memory_space=pltpu.HBM)


def in_hbm(x):
    return pltpu.with_memory_space_constraint(x, pltpu.HBM)


def local_call(kernel, name, out_shape, in_specs, scratch=(), out=WHOLE, **options):
    return pl.pallas_call(
        kernel,
        out_shape=out_shape,
        in_specs=in_specs,
        out_specs=jax.tree.map(lambda _: out, out_shape),
        scratch_shapes=list(scratch),
        compiler_params=pltpu.CompilerParams(vmem_limit_bytes=40 * 2**20),
        name=name,
        **options,
    )


def chain_kernel(raw, swapped, right, left_t, first, second, out):
    bf16 = jnp.bfloat16
    core = lax.axis_index("fsdp")
    lane = number(lax.axis_index("dp"))[1]
    size = raw.shape[1]
    picks = size // 8

    n = iota((256, 256), 0)
    at = ((n >> 2) & 1) * 128 + (n >> 6) * 32 + ((n >> 3) & 7) * 4 + (n & 3)
    pick = one_hot(iota((256, 256), 1) == at)
    low = jnp.where(core == 0, raw[...], swapped[...])
    high = jnp.where(core == 0, swapped[...], raw[...])
    block = []
    for i in range(0, size // 2, 128):
        rows = jnp.concatenate([low[i : i + 128], high[i : i + 128]], axis=0)
        block.append(dot(pick, rows).astype(bf16))
    block = jnp.concatenate(block, axis=0)

    half_rot = dot(left_t[...], block).astype(bf16)
    rotated = dot(half_rot, right[...])
    new_first = adam_first * first[...] + (1.0 - adam_first) * rotated
    new_second = adam_second * second[...] + (1.0 - adam_second) * rotated * rotated
    scaled = (new_first / (jnp.sqrt(new_second) + epsilon)).astype(bf16)
    back = dot(scaled, right[...], 1, 1).astype(bf16)
    update = dot(left_t[...], back, 0, 0)

    own = one_hot(iota((picks, size), 1) == iota((picks, size), 0) * 8 + lane)
    gram_l = dot(dot(own, block).astype(bf16), block, 1, 1).astype(bf16)
    gram_r = dot(dot(block, own, 1, 1).astype(bf16), block, 0, 0).astype(bf16)

    upper = rotated.astype(bf16)
    lower = (rotated - upper.astype(jnp.float32)).astype(bf16)
    rows = jnp.concatenate([gram_l, gram_r, upper, lower], axis=0)
    n, col = iota((size, 4 * picks), 0), iota((size, 4 * picks), 1)
    spread = one_hot(col == ((n & 7) - 4 * (1 - core)) * picks + (n >> 3))
    kept = (iota((size, size), 0) & 4) == 4 * core
    result = jnp.where(kept, update, dot(spread, rows))
    order = [PLACE[b, g] * 8 for b in EIGHT for g in EIGHT]
    out[...] = jnp.concatenate([result[at : at + 8] for at in order], axis=0).astype(bf16)


def chain(raw, *others):
    width = raw.shape[1]
    out = jax.ShapeDtypeStruct((width, width), jnp.bfloat16)
    return local_call(chain_kernel, "block_chain", out, [WHOLE] * 6)(raw, *others)


def finish_kernel(slot_block, home, gram_l, gram_r, first, second, *refs):
    outs, built, sent = refs[:5], refs[5:10], refs[10]
    core = lax.axis_index("fsdp")
    blocks = home.shape[0]
    n, col = iota((32, 64), 0), iota((32, 64), 1)
    kind, chip, row = n >> 3, col >> 3, col & 7
    other = row - 4 * (1 - core)
    product = (chip == (n & 7)) & ((other == kind) | ((kind == 2) & (other == 3)))
    hit = ((kind == 3) & (row - 4 * core == (n & 7))) | ((kind < 3) & product)
    take = one_hot(hit)
    share = jnp.where(slot_block[core, 0] >= 0, 1.0, 0.0)
    copies = []
    for slot in range(blocks):
        block = jnp.maximum(slot_block[0, slot], slot_block[1, slot])
        rows = dot(take, home[block])
        built[4][block] = rows[24:28].astype(jnp.bfloat16)
        rows = rows[:24] * share
        rotated = rows[16:24]
        built[0][slot] = shampoo_beta * gram_l[slot] + (1.0 - shampoo_beta) * rows[:8]
        built[1][slot] = shampoo_beta * gram_r[slot] + (1.0 - shampoo_beta) * rows[8:16]
        built[2][slot] = adam_first * first[slot] + (1.0 - adam_first) * rotated
        built[3][slot] = (
            adam_second * second[slot] + (1.0 - adam_second) * rotated * rotated
        )
        if slot % 4 == 3:
            part = pl.ds(slot - 3, 4)
            for i in range(4):
                copies.append(
                    pltpu.make_async_copy(
                        built[i].at[part], outs[i].at[part], sent.at[i, slot // 4]
                    )
                )
                copies[-1].start()
    copies.append(pltpu.make_async_copy(built[4], outs[4], sent.at[4, 0]))
    copies[-1].start()
    for copy in copies:
        copy.wait()


def finish(slot_block, home, states):
    blocks, width = home.shape[0], home.shape[2]
    outs = [jax.ShapeDtypeStruct(x.shape, x.dtype) for x in states]
    outs.append(jax.ShapeDtypeStruct((blocks, 4, width), jnp.bfloat16))
    return local_call(
        finish_kernel,
        "new_state",
        outs,
        [SCALARS] + [WHOLE] * 5,
        [pltpu.VMEM(x.shape, x.dtype) for x in outs] + [pltpu.SemaphoreType.DMA((5, 2))],
        out=FAR,
    )(slot_block, home, *states)


def on_core(zero, one):
    core = lax.axis_index("fsdp")
    pl.when(core == 0)(zero)
    pl.when(core != 0)(one)


def halves_kernel(left_t, right, first, second, keep, give, *scratch):
    held, done = scratch[:4], scratch[4]
    copies = [
        pltpu.make_async_copy(source, to, done.at[i])
        for i, (source, to) in enumerate(zip((left_t, right, first, second), held))
    ]
    for copy in copies:
        copy.start()
    for copy in copies:
        copy.wait()
    core = lax.axis_index("fsdp")
    for slot in range(keep.shape[0]):
        left_rows, right_rows, one, two = (part[slot].astype(jnp.float32) for part in held)
        upper = one.astype(jnp.bfloat16).astype(jnp.float32)
        whole = jnp.concatenate([right_rows] * 4, axis=0)
        singles = jnp.concatenate([left_rows, upper, one - upper, two], axis=0)
        keep[slot] = jnp.where(core == 0, whole, singles).astype(jnp.bfloat16)
        give[slot] = jnp.where(core == 0, singles, whole).astype(jnp.bfloat16)


def halves(*states):
    blocks, rows, width = states[0].shape
    return local_call(
        halves_kernel,
        "state_halves",
        [jax.ShapeDtypeStruct((blocks, 4 * rows, width), jnp.bfloat16)] * 2,
        [FAR] * 4,
        [pltpu.VMEM(x.shape, x.dtype) for x in states] + [pltpu.SemaphoreType.DMA((4,))],
    )(*states)


def load_kernel(terms, by_block, out, done):
    blocks, chips, span = terms.shape[:3]
    part = chips // 2
    near, cross = [], []
    for b in range(blocks):
        for i in range(2):
            units, some = pl.ds(i * part * span, part * span), pl.ds(i * part, part)
            near.append((by_block.at[b, units], out.at[b, units]))
            cross.append((terms.at[b, some], out.at[some, pl.ds(b * span, span)]))
    near = [pltpu.make_async_copy(*ends, done.at[i]) for i, ends in enumerate(near)]
    cross = [pltpu.make_async_copy(*ends, done.at[i]) for i, ends in enumerate(cross)]
    for one, two in zip(near, cross):
        on_core(one.start, two.start)
    for one, two in zip(near, cross):
        on_core(one.wait, two.wait)


def load(terms):
    blocks, chips, span, rows, width = terms.shape
    return local_call(
        load_kernel,
        "load_terms",
        jax.ShapeDtypeStruct((blocks, chips * span + GROUP, rows, width), terms.dtype),
        [FAR] * 2,
        [pltpu.SemaphoreType.DMA((2 * blocks,))],
        cost_estimate=pl.CostEstimate(flops=0, bytes_accessed=2 * terms.nbytes, transcendentals=0),
    )(in_hbm(terms), in_hbm(terms.reshape(blocks, chips * span, rows, width)))


def pack_kernel(slot_block, loaded, keep, given, out):
    core = lax.axis_index("fsdp")
    blocks = out.shape[0]
    units = out.shape[1] - GROUP
    mine = slot_block[core, 0] >= 0
    n, col = iota((32, 32), 0), iota((32, 32), 1)
    turn = one_hot(col == (n & 3) * 8 + (n >> 2))
    for b in range(blocks):
        at = 0
        for owner in range(slot_block.shape[0]):
            for slot in range(blocks):
                at += jnp.where(slot_block[owner, slot] == b, slot, 0)
        rows = jnp.where(mine, keep[at], given[at])

        def whole(b=b, rows=rows):
            right = rows[:8].astype(jnp.float32)
            out[b, units] = right[:4].astype(jnp.bfloat16)
            out[b, units + 1] = right[4:].astype(jnp.bfloat16)

        def singles(b=b, rows=rows):
            turned = dot(turn, rows).astype(jnp.bfloat16)
            for g in EIGHT:
                out[g, units + b] = turned[4 * g : 4 * g + 4]

        on_core(whole, singles)


def pack(slot_block, loaded, keep, given):
    return local_call(
        pack_kernel,
        "pack_states",
        jax.ShapeDtypeStruct(loaded.shape, loaded.dtype),
        [SCALARS] + [WHOLE] * 3,
        input_output_aliases={1: 0},
    )(slot_block, loaded, keep, given)


def total_of(received, *at):
    return jnp.sum(received[(slice(None), *at)].astype(jnp.float32), axis=0)


def relay_kernel(received, out):
    units = received.shape[1] - GROUP
    span = units // GROUP
    for then in EIGHT:
        for unit in range(span):
            total = total_of(received, then * span + unit)
            out[then, unit] = total.astype(jnp.bfloat16)

    def whole():
        for source in EIGHT:
            for i in range(2):
                rows = received[source, units + i]
                for then in EIGHT:
                    out[then, span + 2 * source + i] = rows

    def singles():
        for source in EIGHT:
            for then in EIGHT:
                out[then, span + source] = received[source, units + then]

    on_core(whole, singles)


def relay(received):
    span = received.shape[1] // GROUP - 1
    shape = (GROUP, span + 2 * GROUP) + received.shape[2:]
    out = jax.ShapeDtypeStruct(shape, received.dtype)
    return local_call(relay_kernel, "relay", out, [WHOLE])(received)


def sum_kernel(received, copies, state):
    span = received.shape[1] - 2 * GROUP
    total = jnp.concatenate([total_of(received, unit) for unit in range(span)], axis=0)
    total = total.astype(jnp.bfloat16)
    for peer in range(copies.shape[0]):
        copies[peer] = total

    def whole():
        for later in EIGHT:
            for early in EIGHT:
                at = span + 2 * early
                pair = [received[later, at + i].astype(jnp.float32) for i in range(2)]
                rows = jnp.concatenate(pair, axis=0)
                state[PLACE[early, later]] = rows.astype(jnp.bfloat16)

    def singles():
        for later in EIGHT:
            for early in EIGHT:
                rows = received[later, span + early].astype(jnp.float32)
                rows = jnp.concatenate([rows, rows], axis=0)
                state[PLACE[later, early]] = rows.astype(jnp.bfloat16)

    on_core(whole, singles)


def sum_terms(received):
    rows, width = received.shape[2:]
    span = received.shape[1] - 2 * GROUP
    outs = [
        jax.ShapeDtypeStruct((GROUP, span * rows, width), received.dtype),
        jax.ShapeDtypeStruct((GROUP * GROUP, 2 * rows, width), received.dtype),
    ]
    return local_call(sum_kernel, "sum_terms", outs, [WHOLE])(received)


def shards(
    grad_parts,
    slot_block,
    gram_left,
    gram_right,
    left_basis_t,
    right_basis,
    moment_first,
    moment_second,
):
    blocks = grad_parts.shape[1]
    q_total = grad_parts.shape[2]
    half_span = grad_parts.shape[3]
    width = grad_parts.shape[4]
    core = lax.axis_index("fsdp")

    states = (left_basis_t, right_basis, moment_first, moment_second)
    states = tuple(in_hbm(part) for part in states)
    terms = grad_parts[0].reshape(blocks, GROUP, q_total // GROUP, half_span, width)
    keep, give = halves(*states)
    message = pack(in_hbm(slot_block), load(terms), keep, swap_cores(give))
    received = exchange(relay(exchange(message, FIRST)), SECOND)
    raw, half = sum_terms(received)
    raw = exchange(raw, BLOCK).reshape(-1, width)

    given = swap_cores(half)
    right = jnp.where(core == 0, half, given).reshape(width, width)
    singles = jnp.where(core == 0, given, half)
    left_t = singles[:, 0]
    first = singles[:, 1].astype(jnp.float32) + singles[:, 2].astype(jnp.float32)
    second = singles[:, 3].astype(jnp.float32)

    home = chain(raw, swap_cores(raw), right, left_t, first, second)
    home = exchange(home.reshape(blocks * GROUP, 8, width), ALL)

    outs = finish(
        slot_block,
        home.reshape(blocks, GROUP * 8, width),
        (gram_left, gram_right, moment_first, moment_second),
    )
    return (*outs[:4], outs[4][:, None])


def solution(mesh):
    state = P("fsdp", "dp", None)
    return jax.shard_map(
        shards,
        mesh=mesh,
        in_specs=(P("dp", None, None, "fsdp", None), P()) + (state,) * 6,
        out_specs=(state,) * 4 + (P(None, "dp", "fsdp", None),),
        check_vma=False,
    )
```

```python
import jax
import jax.numpy as jnp
from jax import lax
from jax.experimental import pallas as pl
from jax.experimental.pallas import tpu as pltpu
from jax.sharding import PartitionSpec as P

shampoo_beta = 0.9
adam_first = 0.95
adam_second = 0.95
epsilon = 1e-08

GROUP = 8
AXES = ("fsdp", "dp")


def number(dp):
    b = g = 0
    for axis in range(3):
        place = (dp >> (2 * axis)) & 3
        wrap, inner = place >> 1, (place ^ (place >> 1)) & 1
        b += (inner if axis == 2 else wrap) << axis
        g += (wrap if axis == 2 else inner) << axis
    return b, g


PLACE = {number(dp): dp for dp in range(GROUP * GROUP)}
EIGHT = range(GROUP)


def device(c, b, g):
    return c * GROUP * GROUP + PLACE[b, g]


OVER_B = [[[device(c, b, g) for b in EIGHT] for g in EIGHT] for c in range(2)]
OVER_G = [[[device(c, b, g) for g in EIGHT] for b in EIGHT] for c in range(2)]
FIRST = OVER_B[0] + OVER_G[1]
SECOND = OVER_G[0] + OVER_B[1]
BLOCK = OVER_G[0] + OVER_G[1]
ALL = [[device(c, b, g) for b in EIGHT for g in EIGHT] for c in range(2)]


def exchange(x, groups):
    return lax.all_to_all(x, AXES, 0, 0, axis_index_groups=groups, tiled=True)


def swap_cores(x):
    return lax.ppermute(x, "fsdp", [(0, 1), (1, 0)])


def dot(a, b, ca=1, cb=0):
    return lax.dot_general(a, b, (((ca,), (cb,)), ((), ())), preferred_element_type=jnp.float32)


def iota(shape, axis):
    return lax.broadcasted_iota(jnp.int32, shape, axis)


def one_hot(hit):
    return jnp.where(hit, 1.0, 0.0).astype(jnp.bfloat16)


WHOLE = pl.BlockSpec(memory_space=pltpu.VMEM)
SCALARS = pl.BlockSpec(memory_space=pltpu.SMEM)
FAR = pl.BlockSpec(memory_space=pltpu.HBM)


def in_hbm(x):
    return pltpu.with_memory_space_constraint(x, pltpu.HBM)


def local_call(kernel, name, out_shape, in_specs, scratch=(), out=WHOLE, **options):
    return pl.pallas_call(
        kernel,
        out_shape=out_shape,
        in_specs=in_specs,
        out_specs=jax.tree.map(lambda _: out, out_shape),
        scratch_shapes=list(scratch),
        compiler_params=pltpu.CompilerParams(vmem_limit_bytes=40 * 2**20),
        name=name,
        **options,
    )


def chain_kernel(raw, swapped, right, left_t, first, second, out):
    bf16 = jnp.bfloat16
    core = lax.axis_index("fsdp")
    lane = number(lax.axis_index("dp"))[1]
    size = raw.shape[1]
    picks = size // 8

    n = iota((256, 256), 0)
    at = ((n >> 2) & 1) * 128 + (n >> 6) * 32 + ((n >> 3) & 7) * 4 + (n & 3)
    pick = one_hot(iota((256, 256), 1) == at)
    low = jnp.where(core == 0, raw[...], swapped[...])
    high = jnp.where(core == 0, swapped[...], raw[...])
    block = []
    for i in range(0, size // 2, 128):
        rows = jnp.concatenate([low[i : i + 128], high[i : i + 128]], axis=0)
        block.append(dot(pick, rows).astype(bf16))
    block = jnp.concatenate(block, axis=0)

    half_rot = dot(left_t[...], block).astype(bf16)
    rotated = dot(half_rot, right[...])
    new_first = adam_first * first[...] + (1.0 - adam_first) * rotated
    new_second = adam_second * second[...] + (1.0 - adam_second) * rotated * rotated
    scaled = (new_first / (jnp.sqrt(new_second) + epsilon)).astype(bf16)
    back = dot(scaled, right[...], 1, 1).astype(bf16)
    update = dot(left_t[...], back, 0, 0)

    own = one_hot(iota((picks, size), 1) == iota((picks, size), 0) * 8 + lane)
    gram_l = dot(dot(own, block).astype(bf16), block, 1, 1).astype(bf16)
    gram_r = dot(dot(block, own, 1, 1).astype(bf16), block, 0, 0).astype(bf16)

    upper = rotated.astype(bf16)
    lower = (rotated - upper.astype(jnp.float32)).astype(bf16)
    rows = jnp.concatenate([gram_l, gram_r, upper, lower], axis=0)
    n, col = iota((size, 4 * picks), 0), iota((size, 4 * picks), 1)
    spread = one_hot(col == ((n & 7) - 4 * (1 - core)) * picks + (n >> 3))
    kept = (iota((size, size), 0) & 4) == 4 * core
    result = jnp.where(kept, update, dot(spread, rows))
    order = [PLACE[b, g] * 8 for b in EIGHT for g in EIGHT]
    out[...] = jnp.concatenate([result[at : at + 8] for at in order], axis=0).astype(bf16)


def chain(raw, *others):
    width = raw.shape[1]
    out = jax.ShapeDtypeStruct((width, width), jnp.bfloat16)
    return local_call(chain_kernel, "block_chain", out, [WHOLE] * 6)(raw, *others)


def finish_kernel(slot_block, home, gram_l, gram_r, first, second, *refs):
    outs, built, sent = refs[:5], refs[5:10], refs[10]
    core = lax.axis_index("fsdp")
    blocks, width = gram_l.shape[0], home.shape[1]
    n, col = iota((24, width), 0), iota((24, width), 1)
    other = (col & 7) - 4 * (1 - core)
    kind = n >> 3
    wanted = (other == kind) | ((kind == 2) & (other == 3))
    picks = []
    for slot in range(blocks):
        block = jnp.maximum(slot_block[core, slot], 0)
        picks.append(one_hot(wanted & ((col >> 3) == block * 8 + (n & 7))))
    share = jnp.where(slot_block[core, 0] >= 0, 1.0, 0.0)
    rows = dot(jnp.concatenate(picks, axis=0), home[...]) * share
    n, col = iota((4 * blocks, width), 0), iota((4 * blocks, width), 1)
    sums = one_hot(((col >> 6) == (n >> 2)) & ((col & 7) - 4 * core == (n & 3)))
    sums = dot(sums, home[...])
    copies = []
    for slot in range(blocks):
        mine = rows[24 * slot : 24 * slot + 24]
        rotated = mine[16:24]
        built[0][slot] = shampoo_beta * gram_l[slot] + (1.0 - shampoo_beta) * mine[:8]
        built[1][slot] = shampoo_beta * gram_r[slot] + (1.0 - shampoo_beta) * mine[8:16]
        built[2][slot] = adam_first * first[slot] + (1.0 - adam_first) * rotated
        built[3][slot] = (
            adam_second * second[slot] + (1.0 - adam_second) * rotated * rotated
        )
        if slot % 4 == 3:
            part = pl.ds(slot - 3, 4)
            for i in range(4):
                copies.append(
                    pltpu.make_async_copy(
                        built[i].at[part], outs[i].at[part], sent.at[i, slot // 4]
                    )
                )
                copies[-1].start()
    for b in range(blocks):
        built[4][b] = sums[4 * b : 4 * b + 4].astype(jnp.bfloat16)
    copies.append(pltpu.make_async_copy(built[4], outs[4], sent.at[4, 0]))
    copies[-1].start()
    for copy in copies:
        copy.wait()


def finish(slot_block, home, states):
    blocks, width = states[0].shape[0], home.shape[1]
    outs = [jax.ShapeDtypeStruct(x.shape, x.dtype) for x in states]
    outs.append(jax.ShapeDtypeStruct((blocks, 4, width), jnp.bfloat16))
    return local_call(
        finish_kernel,
        "new_state",
        outs,
        [SCALARS] + [WHOLE] * 5,
        [pltpu.VMEM(x.shape, x.dtype) for x in outs] + [pltpu.SemaphoreType.DMA((5, 2))],
        out=FAR,
    )(slot_block, home, *states)


def on_core(zero, one):
    core = lax.axis_index("fsdp")
    pl.when(core == 0)(zero)
    pl.when(core != 0)(one)


def halves_kernel(left_t, right, first, second, keep, give, *scratch):
    held, done = scratch[:4], scratch[4]
    copies = [
        pltpu.make_async_copy(source, to, done.at[i])
        for i, (source, to) in enumerate(zip((left_t, right, first, second), held))
    ]
    for copy in copies:
        copy.start()
    for copy in copies:
        copy.wait()
    core = lax.axis_index("fsdp")
    for slot in range(keep.shape[0]):
        left_rows, right_rows, one, two = (part[slot].astype(jnp.float32) for part in held)
        upper = one.astype(jnp.bfloat16).astype(jnp.float32)
        whole = jnp.concatenate([right_rows] * 4, axis=0)
        singles = jnp.concatenate([left_rows, upper, one - upper, two], axis=0)
        keep[slot] = jnp.where(core == 0, whole, singles).astype(jnp.bfloat16)
        give[slot] = jnp.where(core == 0, singles, whole).astype(jnp.bfloat16)


def halves(*states):
    blocks, rows, width = states[0].shape
    return local_call(
        halves_kernel,
        "state_halves",
        [jax.ShapeDtypeStruct((blocks, 4 * rows, width), jnp.bfloat16)] * 2,
        [FAR] * 4,
        [pltpu.VMEM(x.shape, x.dtype) for x in states] + [pltpu.SemaphoreType.DMA((4,))],
    )(*states)


def load_kernel(terms, by_block, out, done):
    blocks, chips, span = terms.shape[:3]
    near = [
        pltpu.make_async_copy(by_block.at[b], out.at[b, pl.ds(0, chips * span)], done.at[b])
        for b in range(blocks)
    ]
    cross = [
        pltpu.make_async_copy(terms.at[b], out.at[:, pl.ds(b * span, span)], done.at[b])
        for b in range(blocks)
    ]
    for b in range(blocks):
        on_core(near[b].start, cross[b].start)
    for b in range(blocks):
        on_core(near[b].wait, cross[b].wait)


def load(terms):
    blocks, chips, span, rows, width = terms.shape
    return local_call(
        load_kernel,
        "load_terms",
        jax.ShapeDtypeStruct((blocks, chips * span + GROUP, rows, width), terms.dtype),
        [FAR] * 2,
        [pltpu.SemaphoreType.DMA((blocks,))],
        cost_estimate=pl.CostEstimate(flops=0, bytes_accessed=2 * terms.nbytes, transcendentals=0),
    )(in_hbm(terms), in_hbm(terms.reshape(blocks, chips * span, rows, width)))


def pack_kernel(slot_block, loaded, keep, given, out):
    core = lax.axis_index("fsdp")
    blocks = out.shape[0]
    units = out.shape[1] - GROUP
    mine = slot_block[core, 0] >= 0
    n, col = iota((32, 32), 0), iota((32, 32), 1)
    turn = one_hot(col == (n & 3) * 8 + (n >> 2))
    for b in range(blocks):
        at = 0
        for owner in range(slot_block.shape[0]):
            for slot in range(blocks):
                at += jnp.where(slot_block[owner, slot] == b, slot, 0)
        rows = jnp.where(mine, keep[at], given[at])

        def whole(b=b, rows=rows):
            right = rows[:8].astype(jnp.float32)
            out[b, units] = right[:4].astype(jnp.bfloat16)
            out[b, units + 1] = right[4:].astype(jnp.bfloat16)

        def singles(b=b, rows=rows):
            turned = dot(turn, rows).astype(jnp.bfloat16)
            for g in EIGHT:
                out[g, units + b] = turned[4 * g : 4 * g + 4]

        on_core(whole, singles)


def pack(slot_block, loaded, keep, given):
    return local_call(
        pack_kernel,
        "pack_states",
        jax.ShapeDtypeStruct(loaded.shape, loaded.dtype),
        [SCALARS] + [WHOLE] * 3,
        input_output_aliases={1: 0},
    )(slot_block, loaded, keep, given)


def total_of(received, *at):
    return jnp.sum(received[(slice(None), *at)].astype(jnp.float32), axis=0)


def relay_kernel(received, out):
    units = received.shape[1] - GROUP
    span = units // GROUP
    for then in EIGHT:
        for unit in range(span):
            total = total_of(received, then * span + unit)
            out[then, unit] = total.astype(jnp.bfloat16)

    def whole():
        for source in EIGHT:
            for i in range(2):
                rows = received[source, units + i]
                for then in EIGHT:
                    out[then, span + 2 * source + i] = rows

    def singles():
        for source in EIGHT:
            for then in EIGHT:
                out[then, span + source] = received[source, units + then]

    on_core(whole, singles)


def relay(received):
    span = received.shape[1] // GROUP - 1
    shape = (GROUP, span + 2 * GROUP) + received.shape[2:]
    out = jax.ShapeDtypeStruct(shape, received.dtype)
    return local_call(relay_kernel, "relay", out, [WHOLE])(received)


def sum_kernel(received, copies, state):
    span = received.shape[1] - 2 * GROUP
    total = jnp.concatenate([total_of(received, unit) for unit in range(span)], axis=0)
    total = total.astype(jnp.bfloat16)
    for peer in range(copies.shape[0]):
        copies[peer] = total

    def whole():
        for later in EIGHT:
            for early in EIGHT:
                for i in range(2):
                    state[PLACE[early, later], i] = received[later, span + 2 * early + i]

    def singles():
        for later in EIGHT:
            for early in EIGHT:
                state[PLACE[later, early], 0] = received[later, span + early]

    on_core(whole, singles)


def sum_terms(received):
    rows, width = received.shape[2:]
    span = received.shape[1] - 2 * GROUP
    outs = [
        jax.ShapeDtypeStruct((GROUP, span * rows, width), received.dtype),
        jax.ShapeDtypeStruct((GROUP * GROUP, 2, rows, width), received.dtype),
    ]
    return local_call(sum_kernel, "sum_terms", outs, [WHOLE])(received)


def shards(
    grad_parts,
    slot_block,
    gram_left,
    gram_right,
    left_basis_t,
    right_basis,
    moment_first,
    moment_second,
):
    blocks = grad_parts.shape[1]
    q_total = grad_parts.shape[2]
    half_span = grad_parts.shape[3]
    width = grad_parts.shape[4]
    core = lax.axis_index("fsdp")

    states = (left_basis_t, right_basis, moment_first, moment_second)
    states = tuple(in_hbm(part) for part in states)
    terms = grad_parts[0].reshape(blocks, GROUP, q_total // GROUP, half_span, width)
    keep, give = halves(*states)
    message = pack(in_hbm(slot_block), load(terms), keep, swap_cores(give))
    received = exchange(relay(exchange(message, FIRST)), SECOND)
    raw, half = sum_terms(received)
    raw = exchange(raw, BLOCK).reshape(-1, width)

    given = swap_cores(half)
    right = jnp.where(core == 0, half, given).reshape(width, width)
    singles = jnp.where(core == 0, given, half)[:, 0]
    left_t = singles[:, 0]
    first = singles[:, 1].astype(jnp.float32) + singles[:, 2].astype(jnp.float32)
    second = singles[:, 3].astype(jnp.float32)

    home = chain(raw, swap_cores(raw), right, left_t, first, second)
    home = exchange(home.reshape(blocks * GROUP, 8, width), ALL)

    outs = finish(
        slot_block,
        home.reshape(width, width),
        (gram_left, gram_right, moment_first, moment_second),
    )
    return (*outs[:4], outs[4][:, None])


def solution(mesh):
    state = P("fsdp", "dp", None)
    return jax.shard_map(
        shards,
        mesh=mesh,
        in_specs=(P("dp", None, None, "fsdp", None), P()) + (state,) * 6,
        out_specs=(state,) * 4 + (P(None, "dp", "fsdp", None),),
        check_vma=False,
    )
```

```python
import jax
import jax.numpy as jnp
from jax import lax
from jax.experimental import pallas as pl
from jax.experimental.pallas import tpu as pltpu
from jax.sharding import PartitionSpec as P

shampoo_beta = 0.9
adam_first = 0.95
adam_second = 0.95
epsilon = 1e-08

GROUP = 8
AXES = ("fsdp", "dp")


def number(dp):
    b = g = 0
    for axis in range(3):
        place = (dp >> (2 * axis)) & 3
        b += (place >> 1) << axis
        g += ((place ^ (place >> 1)) & 1) << axis
    return b, g


PLACE = {number(dp): dp for dp in range(GROUP * GROUP)}
EIGHT = range(GROUP)


def device(c, b, g):
    return c * GROUP * GROUP + PLACE[b, g]


OVER_B = [[[device(c, b, g) for b in EIGHT] for g in EIGHT] for c in range(2)]
OVER_G = [[[device(c, b, g) for g in EIGHT] for b in EIGHT] for c in range(2)]
FIRST = OVER_B[0] + OVER_G[1]
SECOND = OVER_G[0] + OVER_B[1]
BLOCK = OVER_G[0] + OVER_G[1]
ALL = [[device(c, b, g) for b in EIGHT for g in EIGHT] for c in range(2)]


def exchange(x, groups):
    return lax.all_to_all(x, AXES, 0, 0, axis_index_groups=groups, tiled=True)


def swap_cores(x):
    return lax.ppermute(x, "fsdp", [(0, 1), (1, 0)])


def dot(a, b, ca=1, cb=0):
    return lax.dot_general(a, b, (((ca,), (cb,)), ((), ())), preferred_element_type=jnp.float32)


def iota(shape, axis):
    return lax.broadcasted_iota(jnp.int32, shape, axis)


def one_hot(hit):
    return jnp.where(hit, 1.0, 0.0).astype(jnp.bfloat16)


WHOLE = pl.BlockSpec(memory_space=pltpu.VMEM)
SCALARS = pl.BlockSpec(memory_space=pltpu.SMEM)
FAR = pl.BlockSpec(memory_space=pltpu.HBM)


def in_hbm(x):
    return pltpu.with_memory_space_constraint(x, pltpu.HBM)


def local_call(kernel, name, out_shape, in_specs, scratch=(), out=WHOLE, **options):
    return pl.pallas_call(
        kernel,
        out_shape=out_shape,
        in_specs=in_specs,
        out_specs=jax.tree.map(lambda _: out, out_shape),
        scratch_shapes=list(scratch),
        compiler_params=pltpu.CompilerParams(vmem_limit_bytes=40 * 2**20),
        name=name,
        **options,
    )


def chain_kernel(raw, swapped, right, left_t, first, second, out):
    bf16 = jnp.bfloat16
    core = lax.axis_index("fsdp")
    lane = number(lax.axis_index("dp"))[1]
    size = raw.shape[1]
    picks = size // 8

    n = iota((256, 256), 0)
    at = ((n >> 2) & 1) * 128 + (n >> 6) * 32 + ((n >> 3) & 7) * 4 + (n & 3)
    pick = one_hot(iota((256, 256), 1) == at)
    low = jnp.where(core == 0, raw[...], swapped[...])
    high = jnp.where(core == 0, swapped[...], raw[...])
    block = []
    for i in range(0, size // 2, 128):
        rows = jnp.concatenate([low[i : i + 128], high[i : i + 128]], axis=0)
        block.append(dot(pick, rows).astype(bf16))
    block = jnp.concatenate(block, axis=0)

    half_rot = dot(left_t[...], block).astype(bf16)
    rotated = dot(half_rot, right[...])
    new_first = adam_first * first[...] + (1.0 - adam_first) * rotated
    new_second = adam_second * second[...] + (1.0 - adam_second) * rotated * rotated
    scaled = (new_first / (jnp.sqrt(new_second) + epsilon)).astype(bf16)
    back = dot(scaled, right[...], 1, 1).astype(bf16)
    update = dot(left_t[...], back, 0, 0)

    own = one_hot(iota((picks, size), 1) == iota((picks, size), 0) * 8 + lane)
    gram_l = dot(dot(own, block).astype(bf16), block, 1, 1).astype(bf16)
    gram_r = dot(dot(block, own, 1, 1).astype(bf16), block, 0, 0).astype(bf16)

    upper = rotated.astype(bf16)
    lower = (rotated - upper.astype(jnp.float32)).astype(bf16)
    rows = jnp.concatenate([gram_l, gram_r, upper, lower], axis=0)
    n, col = iota((size, 4 * picks), 0), iota((size, 4 * picks), 1)
    spread = one_hot(col == ((n & 7) - 4 * (1 - core)) * picks + (n >> 3))
    kept = (iota((size, size), 0) & 4) == 4 * core
    result = jnp.where(kept, update, dot(spread, rows))
    order = [PLACE[b, g] * 8 for b in EIGHT for g in EIGHT]
    out[...] = jnp.concatenate([result[at : at + 8] for at in order], axis=0).astype(bf16)


def chain(raw, *others):
    width = raw.shape[1]
    out = jax.ShapeDtypeStruct((width, width), jnp.bfloat16)
    return local_call(chain_kernel, "block_chain", out, [WHOLE] * 6)(raw, *others)


def finish_kernel(slot_block, home, gram_l, gram_r, first, second, *refs):
    outs, built, sent = refs[:5], refs[5:10], refs[10]
    core = lax.axis_index("fsdp")
    blocks = home.shape[0]
    n, col = iota((32, 64), 0), iota((32, 64), 1)
    kind, chip, row = n >> 3, col >> 3, col & 7
    other = row - 4 * (1 - core)
    product = (chip == (n & 7)) & ((other == kind) | ((kind == 2) & (other == 3)))
    hit = ((kind == 3) & (row - 4 * core == (n & 7))) | ((kind < 3) & product)
    take = one_hot(hit)
    share = jnp.where(slot_block[core, 0] >= 0, 1.0, 0.0)
    copies = []
    for slot in range(blocks):
        block = jnp.maximum(slot_block[core, slot], 0)
        rows = dot(take, home[block]) * share
        rotated = rows[16:24]
        built[0][slot] = shampoo_beta * gram_l[slot] + (1.0 - shampoo_beta) * rows[:8]
        built[1][slot] = shampoo_beta * gram_r[slot] + (1.0 - shampoo_beta) * rows[8:16]
        built[2][slot] = adam_first * first[slot] + (1.0 - adam_first) * rotated
        built[3][slot] = (
            adam_second * second[slot] + (1.0 - adam_second) * rotated * rotated
        )
        if slot % 4 == 3:
            part = pl.ds(slot - 3, 4)
            for i in range(4):
                copies.append(
                    pltpu.make_async_copy(
                        built[i].at[part], outs[i].at[part], sent.at[i, slot // 4]
                    )
                )
                copies[-1].start()
    for b in range(blocks):
        built[4][b] = dot(take[24:], home[b])[:4].astype(jnp.bfloat16)
    copies.append(pltpu.make_async_copy(built[4], outs[4], sent.at[4, 0]))
    copies[-1].start()
    for copy in copies:
        copy.wait()


def finish(slot_block, home, states):
    blocks, width = home.shape[0], home.shape[2]
    outs = [jax.ShapeDtypeStruct(x.shape, x.dtype) for x in states]
    outs.append(jax.ShapeDtypeStruct((blocks, 4, width), jnp.bfloat16))
    return local_call(
        finish_kernel,
        "new_state",
        outs,
        [SCALARS] + [WHOLE] * 5,
        [pltpu.VMEM(x.shape, x.dtype) for x in outs] + [pltpu.SemaphoreType.DMA((5, 2))],
        out=FAR,
    )(slot_block, home, *states)


def on_core(zero, one):
    core = lax.axis_index("fsdp")
    pl.when(core == 0)(zero)
    pl.when(core != 0)(one)


def halves_kernel(left_t, right, first, second, keep, give, *scratch):
    held, done = scratch[:4], scratch[4]
    copies = [
        pltpu.make_async_copy(source, to, done.at[i])
        for i, (source, to) in enumerate(zip((left_t, right, first, second), held))
    ]
    for copy in copies:
        copy.start()
    for copy in copies:
        copy.wait()
    core = lax.axis_index("fsdp")
    for slot in range(keep.shape[0]):
        left_rows, right_rows, one, two = (part[slot].astype(jnp.float32) for part in held)
        upper = one.astype(jnp.bfloat16).astype(jnp.float32)
        whole = jnp.concatenate([right_rows] * 4, axis=0)
        singles = jnp.concatenate([left_rows, upper, one - upper, two], axis=0)
        keep[slot] = jnp.where(core == 0, whole, singles).astype(jnp.bfloat16)
        give[slot] = jnp.where(core == 0, singles, whole).astype(jnp.bfloat16)


def halves(*states):
    blocks, rows, width = states[0].shape
    return local_call(
        halves_kernel,
        "state_halves",
        [jax.ShapeDtypeStruct((blocks, 4 * rows, width), jnp.bfloat16)] * 2,
        [FAR] * 4,
        [pltpu.VMEM(x.shape, x.dtype) for x in states] + [pltpu.SemaphoreType.DMA((4,))],
    )(*states)


def load_kernel(terms, by_block, out, done):
    blocks, chips, span = terms.shape[:3]
    near = [
        pltpu.make_async_copy(by_block.at[b], out.at[b, pl.ds(0, chips * span)], done.at[b])
        for b in range(blocks)
    ]
    cross = [
        pltpu.make_async_copy(terms.at[b], out.at[:, pl.ds(b * span, span)], done.at[b])
        for b in range(blocks)
    ]
    for b in range(blocks):
        on_core(near[b].start, cross[b].start)
    for b in range(blocks):
        on_core(near[b].wait, cross[b].wait)


def load(terms):
    blocks, chips, span, rows, width = terms.shape
    return local_call(
        load_kernel,
        "load_terms",
        jax.ShapeDtypeStruct((blocks, chips * span + GROUP, rows, width), terms.dtype),
        [FAR] * 2,
        [pltpu.SemaphoreType.DMA((blocks,))],
        cost_estimate=pl.CostEstimate(flops=0, bytes_accessed=2 * terms.nbytes, transcendentals=0),
    )(in_hbm(terms), in_hbm(terms.reshape(blocks, chips * span, rows, width)))


def pack_kernel(slot_block, loaded, keep, given, out):
    core = lax.axis_index("fsdp")
    blocks = out.shape[0]
    units = out.shape[1] - GROUP
    mine = slot_block[core, 0] >= 0
    n, col = iota((32, 32), 0), iota((32, 32), 1)
    turn = one_hot(col == (n & 3) * 8 + (n >> 2))
    for b in range(blocks):
        at = 0
        for owner in range(slot_block.shape[0]):
            for slot in range(blocks):
                at += jnp.where(slot_block[owner, slot] == b, slot, 0)
        rows = jnp.where(mine, keep[at], given[at])

        def whole(b=b, rows=rows):
            right = rows[:8].astype(jnp.float32)
            out[b, units] = right[:4].astype(jnp.bfloat16)
            out[b, units + 1] = right[4:].astype(jnp.bfloat16)

        def singles(b=b, rows=rows):
            turned = dot(turn, rows).astype(jnp.bfloat16)
            for g in EIGHT:
                out[g, units + b] = turned[4 * g : 4 * g + 4]

        on_core(whole, singles)


def pack(slot_block, loaded, keep, given):
    return local_call(
        pack_kernel,
        "pack_states",
        jax.ShapeDtypeStruct(loaded.shape, loaded.dtype),
        [SCALARS] + [WHOLE] * 3,
        input_output_aliases={1: 0},
    )(slot_block, loaded, keep, given)


def total_of(received, *at):
    return jnp.sum(received[(slice(None), *at)].astype(jnp.float32), axis=0)


def relay_kernel(received, out):
    units = received.shape[1] - GROUP
    span = units // GROUP
    for then in EIGHT:
        for unit in range(span):
            total = total_of(received, then * span + unit)
            out[then, unit] = total.astype(jnp.bfloat16)

    def whole():
        for source in EIGHT:
            for i in range(2):
                rows = received[source, units + i]
                for then in EIGHT:
                    out[then, span + 2 * source + i] = rows

    def singles():
        for source in EIGHT:
            for then in EIGHT:
                out[then, span + source] = received[source, units + then]

    on_core(whole, singles)


def relay(received):
    span = received.shape[1] // GROUP - 1
    shape = (GROUP, span + 2 * GROUP) + received.shape[2:]
    out = jax.ShapeDtypeStruct(shape, received.dtype)
    return local_call(relay_kernel, "relay", out, [WHOLE])(received)


def sum_kernel(received, copies, state):
    span = received.shape[1] - 2 * GROUP
    total = jnp.concatenate([total_of(received, unit) for unit in range(span)], axis=0)
    total = total.astype(jnp.bfloat16)
    for peer in range(copies.shape[0]):
        copies[peer] = total

    def whole():
        for later in EIGHT:
            for early in EIGHT:
                for i in range(2):
                    state[PLACE[early, later], i] = received[later, span + 2 * early + i]

    def singles():
        for later in EIGHT:
            for early in EIGHT:
                state[PLACE[later, early], 0] = received[later, span + early]

    on_core(whole, singles)


def sum_terms(received):
    rows, width = received.shape[2:]
    span = received.shape[1] - 2 * GROUP
    outs = [
        jax.ShapeDtypeStruct((GROUP, span * rows, width), received.dtype),
        jax.ShapeDtypeStruct((GROUP * GROUP, 2, rows, width), received.dtype),
    ]
    return local_call(sum_kernel, "sum_terms", outs, [WHOLE])(received)


def shards(
    grad_parts,
    slot_block,
    gram_left,
    gram_right,
    left_basis_t,
    right_basis,
    moment_first,
    moment_second,
):
    blocks = grad_parts.shape[1]
    q_total = grad_parts.shape[2]
    half_span = grad_parts.shape[3]
    width = grad_parts.shape[4]
    core = lax.axis_index("fsdp")

    states = (left_basis_t, right_basis, moment_first, moment_second)
    states = tuple(in_hbm(part) for part in states)
    terms = grad_parts[0].reshape(blocks, GROUP, q_total // GROUP, half_span, width)
    keep, give = halves(*states)
    message = pack(in_hbm(slot_block), load(terms), keep, swap_cores(give))
    received = exchange(relay(exchange(message, FIRST)), SECOND)
    raw, half = sum_terms(received)
    raw = exchange(raw, BLOCK).reshape(-1, width)

    given = swap_cores(half)
    right = jnp.where(core == 0, half, given).reshape(width, width)
    singles = jnp.where(core == 0, given, half)[:, 0]
    left_t = singles[:, 0]
    first = singles[:, 1].astype(jnp.float32) + singles[:, 2].astype(jnp.float32)
    second = singles[:, 3].astype(jnp.float32)

    home = chain(raw, swap_cores(raw), right, left_t, first, second)
    home = exchange(home.reshape(blocks * GROUP, 8, width), ALL)

    outs = finish(
        slot_block,
        home.reshape(blocks, GROUP * 8, width),
        (gram_left, gram_right, moment_first, moment_second),
    )
    return (*outs[:4], outs[4][:, None])


def solution(mesh):
    state = P("fsdp", "dp", None)
    return jax.shard_map(
        shards,
        mesh=mesh,
        in_specs=(P("dp", None, None, "fsdp", None), P()) + (state,) * 6,
        out_specs=(state,) * 4 + (P(None, "dp", "fsdp", None),),
        check_vma=False,
    )
```

```python
import jax
import jax.numpy as jnp
from jax import lax
from jax.experimental import pallas as pl
from jax.experimental.pallas import tpu as pltpu
from jax.sharding import PartitionSpec as P

shampoo_beta = 0.9
adam_first = 0.95
adam_second = 0.95
epsilon = 1e-08

GROUP = 8
AXES = ("fsdp", "dp")


def number(dp):
    b = g = 0
    for axis in range(3):
        place = (dp >> (2 * axis)) & 3
        wrap, inner = place >> 1, (place ^ (place >> 1)) & 1
        b += (inner if axis == 2 else wrap) << axis
        g += (wrap if axis == 2 else inner) << axis
    return b, g


PLACE = {number(dp): dp for dp in range(GROUP * GROUP)}
EIGHT = range(GROUP)


def device(c, b, g):
    return c * GROUP * GROUP + PLACE[b, g]


OVER_B = [[[device(c, b, g) for b in EIGHT] for g in EIGHT] for c in range(2)]
OVER_G = [[[device(c, b, g) for g in EIGHT] for b in EIGHT] for c in range(2)]
FIRST = OVER_B[0] + OVER_G[1]
SECOND = OVER_G[0] + OVER_B[1]
BLOCK = OVER_G[0] + OVER_G[1]
ALL = [[device(c, b, g) for b in EIGHT for g in EIGHT] for c in range(2)]


def exchange(x, groups):
    return lax.all_to_all(x, AXES, 0, 0, axis_index_groups=groups, tiled=True)


def swap_cores(x):
    return lax.ppermute(x, "fsdp", [(0, 1), (1, 0)])


def dot(a, b, ca=1, cb=0):
    return lax.dot_general(a, b, (((ca,), (cb,)), ((), ())), preferred_element_type=jnp.float32)


def iota(shape, axis):
    return lax.broadcasted_iota(jnp.int32, shape, axis)


def one_hot(hit):
    return jnp.where(hit, 1.0, 0.0).astype(jnp.bfloat16)


WHOLE = pl.BlockSpec(memory_space=pltpu.VMEM)
SCALARS = pl.BlockSpec(memory_space=pltpu.SMEM)
FAR = pl.BlockSpec(memory_space=pltpu.HBM)


def in_hbm(x):
    return pltpu.with_memory_space_constraint(x, pltpu.HBM)


def local_call(kernel, name, out_shape, in_specs, scratch=(), out=WHOLE, **options):
    return pl.pallas_call(
        kernel,
        out_shape=out_shape,
        in_specs=in_specs,
        out_specs=jax.tree.map(lambda _: out, out_shape),
        scratch_shapes=list(scratch),
        compiler_params=pltpu.CompilerParams(vmem_limit_bytes=40 * 2**20),
        name=name,
        **options,
    )


def chain_kernel(raw, swapped, right, left_t, first, second, out):
    bf16 = jnp.bfloat16
    core = lax.axis_index("fsdp")
    lane = number(lax.axis_index("dp"))[1]
    size = raw.shape[1]
    picks = size // 8

    n = iota((256, 256), 0)
    at = ((n >> 2) & 1) * 128 + (n >> 6) * 32 + ((n >> 3) & 7) * 4 + (n & 3)
    pick = one_hot(iota((256, 256), 1) == at)
    low = jnp.where(core == 0, raw[...], swapped[...])
    high = jnp.where(core == 0, swapped[...], raw[...])
    block = []
    for i in range(0, size // 2, 128):
        rows = jnp.concatenate([low[i : i + 128], high[i : i + 128]], axis=0)
        block.append(dot(pick, rows).astype(bf16))
    block = jnp.concatenate(block, axis=0)

    half_rot = dot(left_t[...], block).astype(bf16)
    rotated = dot(half_rot, right[...])
    new_first = adam_first * first[...] + (1.0 - adam_first) * rotated
    new_second = adam_second * second[...] + (1.0 - adam_second) * rotated * rotated
    scaled = (new_first / (jnp.sqrt(new_second) + epsilon)).astype(bf16)
    back = dot(scaled, right[...], 1, 1).astype(bf16)
    update = dot(left_t[...], back, 0, 0)

    own = one_hot(iota((picks, size), 1) == iota((picks, size), 0) * 8 + lane)
    gram_l = dot(dot(own, block).astype(bf16), block, 1, 1).astype(bf16)
    gram_r = dot(dot(block, own, 1, 1).astype(bf16), block, 0, 0).astype(bf16)

    upper = rotated.astype(bf16)
    lower = (rotated - upper.astype(jnp.float32)).astype(bf16)
    rows = jnp.concatenate([gram_l, gram_r, upper, lower], axis=0)
    n, col = iota((size, 4 * picks), 0), iota((size, 4 * picks), 1)
    spread = one_hot(col == ((n & 7) - 4 * (1 - core)) * picks + (n >> 3))
    kept = (iota((size, size), 0) & 4) == 4 * core
    result = jnp.where(kept, update, dot(spread, rows))
    order = [PLACE[b, g] * 8 for b in EIGHT for g in EIGHT]
    out[...] = jnp.concatenate([result[at : at + 8] for at in order], axis=0).astype(bf16)


def chain(raw, *others):
    width = raw.shape[1]
    out = jax.ShapeDtypeStruct((width, width), jnp.bfloat16)
    return local_call(chain_kernel, "block_chain", out, [WHOLE] * 6)(raw, *others)


def finish_kernel(slot_block, home, gram_l, gram_r, first, second, *refs):
    outs, built, sent = refs[:5], refs[5:10], refs[10]
    core = lax.axis_index("fsdp")
    blocks = home.shape[0]
    n, col = iota((32, 64), 0), iota((32, 64), 1)
    kind, chip, row = n >> 3, col >> 3, col & 7
    other = row - 4 * (1 - core)
    product = (chip == (n & 7)) & ((other == kind) | ((kind == 2) & (other == 3)))
    hit = ((kind == 3) & (row - 4 * core == (n & 7))) | ((kind < 3) & product)
    take = one_hot(hit)
    share = jnp.where(slot_block[core, 0] >= 0, 1.0, 0.0)
    copies = []
    for slot in range(blocks):
        block = jnp.maximum(slot_block[core, slot], 0)
        rows = dot(take, home[block]) * share
        rotated = rows[16:24]
        built[0][slot] = shampoo_beta * gram_l[slot] + (1.0 - shampoo_beta) * rows[:8]
        built[1][slot] = shampoo_beta * gram_r[slot] + (1.0 - shampoo_beta) * rows[8:16]
        built[2][slot] = adam_first * first[slot] + (1.0 - adam_first) * rotated
        built[3][slot] = (
            adam_second * second[slot] + (1.0 - adam_second) * rotated * rotated
        )
        if slot % 4 == 3:
            part = pl.ds(slot - 3, 4)
            for i in range(4):
                copies.append(
                    pltpu.make_async_copy(
                        built[i].at[part], outs[i].at[part], sent.at[i, slot // 4]
                    )
                )
                copies[-1].start()
    for b in range(blocks):
        built[4][b] = dot(take[24:], home[b])[:4].astype(jnp.bfloat16)
    copies.append(pltpu.make_async_copy(built[4], outs[4], sent.at[4, 0]))
    copies[-1].start()
    for copy in copies:
        copy.wait()


def finish(slot_block, home, states):
    blocks, width = home.shape[0], home.shape[2]
    outs = [jax.ShapeDtypeStruct(x.shape, x.dtype) for x in states]
    outs.append(jax.ShapeDtypeStruct((blocks, 4, width), jnp.bfloat16))
    return local_call(
        finish_kernel,
        "new_state",
        outs,
        [SCALARS] + [WHOLE] * 5,
        [pltpu.VMEM(x.shape, x.dtype) for x in outs] + [pltpu.SemaphoreType.DMA((5, 2))],
        out=FAR,
    )(slot_block, home, *states)


def on_core(zero, one):
    core = lax.axis_index("fsdp")
    pl.when(core == 0)(zero)
    pl.when(core != 0)(one)


EARLY = 3


def term_copies(terms, by_block, out, done, which):
    chips, span = terms.shape[1:3]
    near = [
        pltpu.make_async_copy(by_block.at[b], out.at[b, pl.ds(0, chips * span)], done.at[b])
        for b in which
    ]
    cross = [
        pltpu.make_async_copy(terms.at[b], out.at[:, pl.ds(b * span, span)], done.at[b])
        for b in which
    ]
    return list(zip(near, cross))


def fill_half(out, held, whole):
    left_t, right, first, second = held
    for slot in range(out.shape[0]):
        rows = [part[slot].astype(jnp.float32) for part in (left_t, right, first, second)]
        upper = rows[2].astype(jnp.bfloat16).astype(jnp.float32)
        singles = jnp.concatenate([rows[0], upper, rows[2] - upper, rows[3]], axis=0)
        right_rows = jnp.concatenate([rows[1]] * 4, axis=0)
        out[slot] = jnp.where(whole, right_rows, singles).astype(jnp.bfloat16)


def fetch(states, held, done):
    copies = [
        pltpu.make_async_copy(source, to, done.at[i])
        for i, (source, to) in enumerate(zip(states, held))
    ]
    for copy in copies:
        copy.start()
    return copies


def start_kernel(terms, by_block, *refs):
    states, out, give, held, done, landed = refs[:4], refs[4], refs[5], refs[6:10], refs[10], refs[11]
    copies = fetch(states, held, landed)
    early = term_copies(terms, by_block, out, done, range(EARLY))
    for near, cross in early:
        on_core(near.start, cross.start)
    for copy in copies:
        copy.wait()
    fill_half(give, held, lax.axis_index("fsdp") == 1)
    for near, cross in early:
        on_core(near.wait, cross.wait)


def load_kernel(loaded, terms, by_block, *refs):
    states, out, keep, held, done, landed = refs[:4], refs[4], refs[5], refs[6:10], refs[10], refs[11]
    copies = fetch(states, held, landed)
    late = term_copies(terms, by_block, out, done, range(EARLY, terms.shape[0]))
    for near, cross in late:
        on_core(near.start, cross.start)
    for copy in copies:
        copy.wait()
    fill_half(keep, held, lax.axis_index("fsdp") == 0)
    for near, cross in late:
        on_core(near.wait, cross.wait)


def prepare(terms, states):
    blocks, chips, span, rows, width = terms.shape
    sources = [in_hbm(terms), in_hbm(terms.reshape(blocks, chips * span, rows, width))]
    sources += map(in_hbm, states)
    shape = (blocks, chips * span + GROUP, rows, width)
    outs = [
        jax.ShapeDtypeStruct(shape, terms.dtype),
        jax.ShapeDtypeStruct((blocks, 4 * states[0].shape[1], width), jnp.bfloat16),
    ]
    scratch = [pltpu.VMEM(x.shape, x.dtype) for x in states]
    scratch += [pltpu.SemaphoreType.DMA((blocks,)), pltpu.SemaphoreType.DMA((4,))]
    loaded, give = local_call(start_kernel, "start_terms", outs, [FAR] * 6, scratch)(*sources)
    given = swap_cores(give)
    loaded, keep = local_call(
        load_kernel,
        "load_terms",
        outs,
        [WHOLE] + [FAR] * 6,
        scratch,
        input_output_aliases={0: 0},
        cost_estimate=pl.CostEstimate(flops=0, bytes_accessed=2 * terms.nbytes, transcendentals=0),
    )(loaded, *sources)
    return loaded, keep, given


def pack_kernel(slot_block, loaded, keep, given, out):
    core = lax.axis_index("fsdp")
    blocks = out.shape[0]
    units = out.shape[1] - GROUP
    mine = slot_block[core, 0] >= 0
    n, col = iota((32, 32), 0), iota((32, 32), 1)
    turn = one_hot(col == (n & 3) * 8 + (n >> 2))
    for b in range(blocks):
        at = 0
        for owner in range(slot_block.shape[0]):
            for slot in range(blocks):
                at += jnp.where(slot_block[owner, slot] == b, slot, 0)
        rows = jnp.where(mine, keep[at], given[at])

        def whole(b=b, rows=rows):
            right = rows[:8].astype(jnp.float32)
            out[b, units] = right[:4].astype(jnp.bfloat16)
            out[b, units + 1] = right[4:].astype(jnp.bfloat16)

        def singles(b=b, rows=rows):
            turned = dot(turn, rows).astype(jnp.bfloat16)
            for g in EIGHT:
                out[g, units + b] = turned[4 * g : 4 * g + 4]

        on_core(whole, singles)


def pack(slot_block, loaded, keep, given):
    return local_call(
        pack_kernel,
        "pack_states",
        jax.ShapeDtypeStruct(loaded.shape, loaded.dtype),
        [SCALARS] + [WHOLE] * 3,
        input_output_aliases={1: 0},
    )(slot_block, loaded, keep, given)


def total_of(received, *at):
    return jnp.sum(received[(slice(None), *at)].astype(jnp.float32), axis=0)


def relay_kernel(received, out):
    units = received.shape[1] - GROUP
    span = units // GROUP
    for then in EIGHT:
        for unit in range(span):
            total = total_of(received, then * span + unit)
            out[then, unit] = total.astype(jnp.bfloat16)

    def whole():
        for source in EIGHT:
            for i in range(2):
                rows = received[source, units + i]
                for then in EIGHT:
                    out[then, span + 2 * source + i] = rows

    def singles():
        for source in EIGHT:
            for then in EIGHT:
                out[then, span + source] = received[source, units + then]

    on_core(whole, singles)


def relay(received):
    span = received.shape[1] // GROUP - 1
    shape = (GROUP, span + 2 * GROUP) + received.shape[2:]
    out = jax.ShapeDtypeStruct(shape, received.dtype)
    return local_call(relay_kernel, "relay", out, [WHOLE])(received)


def sum_kernel(received, copies, state):
    span = received.shape[1] - 2 * GROUP
    total = jnp.concatenate([total_of(received, unit) for unit in range(span)], axis=0)
    total = total.astype(jnp.bfloat16)
    for peer in range(copies.shape[0]):
        copies[peer] = total

    def whole():
        for later in EIGHT:
            for early in EIGHT:
                for i in range(2):
                    state[PLACE[early, later], i] = received[later, span + 2 * early + i]

    def singles():
        for later in EIGHT:
            for early in EIGHT:
                state[PLACE[later, early], 0] = received[later, span + early]

    on_core(whole, singles)


def sum_terms(received):
    rows, width = received.shape[2:]
    span = received.shape[1] - 2 * GROUP
    outs = [
        jax.ShapeDtypeStruct((GROUP, span * rows, width), received.dtype),
        jax.ShapeDtypeStruct((GROUP * GROUP, 2, rows, width), received.dtype),
    ]
    return local_call(sum_kernel, "sum_terms", outs, [WHOLE])(received)


def shards(
    grad_parts,
    slot_block,
    gram_left,
    gram_right,
    left_basis_t,
    right_basis,
    moment_first,
    moment_second,
):
    blocks = grad_parts.shape[1]
    q_total = grad_parts.shape[2]
    half_span = grad_parts.shape[3]
    width = grad_parts.shape[4]
    core = lax.axis_index("fsdp")

    states = (left_basis_t, right_basis, moment_first, moment_second)
    terms = grad_parts[0].reshape(blocks, GROUP, q_total // GROUP, half_span, width)
    message = pack(in_hbm(slot_block), *prepare(terms, states))
    received = exchange(relay(exchange(message, FIRST)), SECOND)
    raw, half = sum_terms(received)
    raw = exchange(raw, BLOCK).reshape(-1, width)

    given = swap_cores(half)
    right = jnp.where(core == 0, half, given).reshape(width, width)
    singles = jnp.where(core == 0, given, half)[:, 0]
    left_t = singles[:, 0]
    first = singles[:, 1].astype(jnp.float32) + singles[:, 2].astype(jnp.float32)
    second = singles[:, 3].astype(jnp.float32)

    home = chain(raw, swap_cores(raw), right, left_t, first, second)
    home = exchange(home.reshape(blocks * GROUP, 8, width), ALL)

    outs = finish(
        slot_block,
        home.reshape(blocks, GROUP * 8, width),
        (gram_left, gram_right, moment_first, moment_second),
    )
    return (*outs[:4], outs[4][:, None])


def solution(mesh):
    state = P("fsdp", "dp", None)
    return jax.shard_map(
        shards,
        mesh=mesh,
        in_specs=(P("dp", None, None, "fsdp", None), P()) + (state,) * 6,
        out_specs=(state,) * 4 + (P(None, "dp", "fsdp", None),),
        check_vma=False,
    )
```

```python
import jax
import jax.numpy as jnp
from jax import lax
from jax.experimental import pallas as pl
from jax.experimental.pallas import tpu as pltpu
from jax.sharding import PartitionSpec as P

shampoo_beta = 0.9
adam_first = 0.95
adam_second = 0.95
epsilon = 1e-08

GROUP = 8
AXES = ("fsdp", "dp")


def number(dp):
    b = g = 0
    for axis in range(3):
        place = (dp >> (2 * axis)) & 3
        wrap, inner = place >> 1, (place ^ (place >> 1)) & 1
        b += (inner if axis == 2 else wrap) << axis
        g += (wrap if axis == 2 else inner) << axis
    return b, g


PLACE = {number(dp): dp for dp in range(GROUP * GROUP)}
EIGHT = range(GROUP)


def device(c, b, g):
    return c * GROUP * GROUP + PLACE[b, g]


OVER_B = [[[device(c, b, g) for b in EIGHT] for g in EIGHT] for c in range(2)]
OVER_G = [[[device(c, b, g) for g in EIGHT] for b in EIGHT] for c in range(2)]
FIRST = OVER_B[0] + OVER_G[1]
SECOND = OVER_G[0] + OVER_B[1]
BLOCK = OVER_G[0] + OVER_G[1]
ALL = [[c * GROUP * GROUP + dp for dp in range(GROUP * GROUP)] for c in range(2)]


def exchange(x, groups):
    return lax.all_to_all(x, AXES, 0, 0, axis_index_groups=groups, tiled=True)


def swap_cores(x):
    return lax.ppermute(x, "fsdp", [(0, 1), (1, 0)])


def dot(a, b, ca=1, cb=0):
    return lax.dot_general(a, b, (((ca,), (cb,)), ((), ())), preferred_element_type=jnp.float32)


def iota(shape, axis):
    return lax.broadcasted_iota(jnp.int32, shape, axis)


def one_hot(hit):
    return jnp.where(hit, 1.0, 0.0).astype(jnp.bfloat16)


WHOLE = pl.BlockSpec(memory_space=pltpu.VMEM)
SCALARS = pl.BlockSpec(memory_space=pltpu.SMEM)
FAR = pl.BlockSpec(memory_space=pltpu.HBM)


def in_hbm(x):
    return pltpu.with_memory_space_constraint(x, pltpu.HBM)


def local_call(kernel, name, out_shape, in_specs, scratch=(), out=WHOLE, **options):
    return pl.pallas_call(
        kernel,
        out_shape=out_shape,
        in_specs=in_specs,
        out_specs=jax.tree.map(lambda _: out, out_shape),
        scratch_shapes=list(scratch),
        compiler_params=pltpu.CompilerParams(vmem_limit_bytes=40 * 2**20),
        name=name,
        **options,
    )


def chain_kernel(raw, swapped, right, left_t, first, second, out):
    bf16 = jnp.bfloat16
    core = lax.axis_index("fsdp")
    lane = number(lax.axis_index("dp"))[1]
    size = raw.shape[1]
    picks = size // 8

    n = iota((256, 256), 0)
    at = ((n >> 2) & 1) * 128 + (n >> 6) * 32 + ((n >> 3) & 7) * 4 + (n & 3)
    pick = one_hot(iota((256, 256), 1) == at)
    low = jnp.where(core == 0, raw[...], swapped[...])
    high = jnp.where(core == 0, swapped[...], raw[...])
    block = []
    for i in range(0, size // 2, 128):
        rows = jnp.concatenate([low[i : i + 128], high[i : i + 128]], axis=0)
        block.append(dot(pick, rows).astype(bf16))
    block = jnp.concatenate(block, axis=0)

    half_rot = dot(left_t[...], block).astype(bf16)
    rotated = dot(half_rot, right[...])
    new_first = adam_first * first[...] + (1.0 - adam_first) * rotated
    new_second = adam_second * second[...] + (1.0 - adam_second) * rotated * rotated
    scaled = (new_first / (jnp.sqrt(new_second) + epsilon)).astype(bf16)
    back = dot(scaled, right[...], 1, 1).astype(bf16)
    update = dot(left_t[...], back, 0, 0)

    own = one_hot(iota((picks, size), 1) == iota((picks, size), 0) * 8 + lane)
    gram_l = dot(dot(own, block).astype(bf16), block, 1, 1).astype(bf16)
    gram_r = dot(dot(block, own, 1, 1).astype(bf16), block, 0, 0).astype(bf16)

    upper = rotated.astype(bf16)
    lower = (rotated - upper.astype(jnp.float32)).astype(bf16)
    rows = jnp.concatenate([gram_l, gram_r, upper, lower], axis=0)
    n, col = iota((size, 4 * picks), 0), iota((size, 4 * picks), 1)
    spread = one_hot(col == ((n & 7) - 4 * (1 - core)) * picks + (n >> 3))
    kept = (iota((size, size), 0) & 4) == 4 * core
    out[...] = jnp.where(kept, update, dot(spread, rows)).astype(bf16)


def chain(raw, *others):
    width = raw.shape[1]
    out = jax.ShapeDtypeStruct((width, width), jnp.bfloat16)
    return local_call(chain_kernel, "block_chain", out, [WHOLE] * 6)(raw, *others)


def finish_kernel(slot_block, home, gram_l, gram_r, first, second, *refs):
    outs, built, sent = refs[:5], refs[5:10], refs[10]
    core = lax.axis_index("fsdp")
    blocks, width = gram_l.shape[0], home.shape[1]
    n, col = iota((24, width), 0), iota((24, width), 1)
    other = (col & 7) - 4 * (1 - core)
    kind = n >> 3
    source, lane = number(col >> 3)
    wanted = ((other == kind) | ((kind == 2) & (other == 3))) & (lane == (n & 7))
    picks = []
    for slot in range(blocks):
        block = jnp.maximum(slot_block[core, slot], 0)
        picks.append(one_hot(wanted & (source == block)))
    share = jnp.where(slot_block[core, 0] >= 0, 1.0, 0.0)
    rows = dot(jnp.concatenate(picks, axis=0), home[...]) * share
    n, col = iota((4 * blocks, width), 0), iota((4 * blocks, width), 1)
    source = number(col >> 3)[0]
    sums = one_hot((source == (n >> 2)) & ((col & 7) - 4 * core == (n & 3)))
    sums = dot(sums, home[...])
    copies = []
    for slot in range(blocks):
        mine = rows[24 * slot : 24 * slot + 24]
        rotated = mine[16:24]
        built[0][slot] = shampoo_beta * gram_l[slot] + (1.0 - shampoo_beta) * mine[:8]
        built[1][slot] = shampoo_beta * gram_r[slot] + (1.0 - shampoo_beta) * mine[8:16]
        built[2][slot] = adam_first * first[slot] + (1.0 - adam_first) * rotated
        built[3][slot] = (
            adam_second * second[slot] + (1.0 - adam_second) * rotated * rotated
        )
        if slot % 4 == 3:
            part = pl.ds(slot - 3, 4)
            for i in range(4):
                copies.append(
                    pltpu.make_async_copy(
                        built[i].at[part], outs[i].at[part], sent.at[i, slot // 4]
                    )
                )
                copies[-1].start()
    for b in range(blocks):
        built[4][b] = sums[4 * b : 4 * b + 4].astype(jnp.bfloat16)
    copies.append(pltpu.make_async_copy(built[4], outs[4], sent.at[4, 0]))
    copies[-1].start()
    for copy in copies:
        copy.wait()


def finish(slot_block, home, states):
    blocks, width = states[0].shape[0], home.shape[1]
    outs = [jax.ShapeDtypeStruct(x.shape, x.dtype) for x in states]
    outs.append(jax.ShapeDtypeStruct((blocks, 4, width), jnp.bfloat16))
    return local_call(
        finish_kernel,
        "new_state",
        outs,
        [SCALARS] + [WHOLE] * 5,
        [pltpu.VMEM(x.shape, x.dtype) for x in outs] + [pltpu.SemaphoreType.DMA((5, 2))],
        out=FAR,
    )(slot_block, home, *states)


def on_core(zero, one):
    core = lax.axis_index("fsdp")
    pl.when(core == 0)(zero)
    pl.when(core != 0)(one)


def halves_kernel(left_t, right, first, second, keep, give, *scratch):
    held, done = scratch[:4], scratch[4]
    copies = [
        pltpu.make_async_copy(source, to, done.at[i])
        for i, (source, to) in enumerate(zip((left_t, right, first, second), held))
    ]
    for copy in copies:
        copy.start()
    for copy in copies:
        copy.wait()
    core = lax.axis_index("fsdp")
    for slot in range(keep.shape[0]):
        left_rows, right_rows, one, two = (part[slot].astype(jnp.float32) for part in held)
        upper = one.astype(jnp.bfloat16).astype(jnp.float32)
        whole = jnp.concatenate([right_rows] * 4, axis=0)
        singles = jnp.concatenate([left_rows, upper, one - upper, two], axis=0)
        keep[slot] = jnp.where(core == 0, whole, singles).astype(jnp.bfloat16)
        give[slot] = jnp.where(core == 0, singles, whole).astype(jnp.bfloat16)


def halves(*states):
    blocks, rows, width = states[0].shape
    return local_call(
        halves_kernel,
        "state_halves",
        [jax.ShapeDtypeStruct((blocks, 4 * rows, width), jnp.bfloat16)] * 2,
        [FAR] * 4,
        [pltpu.VMEM(x.shape, x.dtype) for x in states] + [pltpu.SemaphoreType.DMA((4,))],
    )(*states)


def load_kernel(terms, by_block, out, done):
    blocks, chips, span = terms.shape[:3]
    near = [
        pltpu.make_async_copy(by_block.at[b], out.at[b, pl.ds(0, chips * span)], done.at[b])
        for b in range(blocks)
    ]
    cross = [
        pltpu.make_async_copy(terms.at[b], out.at[:, pl.ds(b * span, span)], done.at[b])
        for b in range(blocks)
    ]
    for b in range(blocks):
        on_core(near[b].start, cross[b].start)
    for b in range(blocks):
        on_core(near[b].wait, cross[b].wait)


def load(terms):
    blocks, chips, span, rows, width = terms.shape
    return local_call(
        load_kernel,
        "load_terms",
        jax.ShapeDtypeStruct((blocks, chips * span + GROUP, rows, width), terms.dtype),
        [FAR] * 2,
        [pltpu.SemaphoreType.DMA((blocks,))],
        cost_estimate=pl.CostEstimate(flops=0, bytes_accessed=2 * terms.nbytes, transcendentals=0),
    )(in_hbm(terms), in_hbm(terms.reshape(blocks, chips * span, rows, width)))


def pack_kernel(slot_block, loaded, keep, given, out):
    core = lax.axis_index("fsdp")
    blocks = out.shape[0]
    units = out.shape[1] - GROUP
    mine = slot_block[core, 0] >= 0
    n, col = iota((32, 32), 0), iota((32, 32), 1)
    turn = one_hot(col == (n & 3) * 8 + (n >> 2))
    for b in range(blocks):
        at = 0
        for owner in range(slot_block.shape[0]):
            for slot in range(blocks):
                at += jnp.where(slot_block[owner, slot] == b, slot, 0)
        rows = jnp.where(mine, keep[at], given[at])

        def whole(b=b, rows=rows):
            right = rows[:8].astype(jnp.float32)
            out[b, units] = right[:4].astype(jnp.bfloat16)
            out[b, units + 1] = right[4:].astype(jnp.bfloat16)

        def singles(b=b, rows=rows):
            turned = dot(turn, rows).astype(jnp.bfloat16)
            for g in EIGHT:
                out[g, units + b] = turned[4 * g : 4 * g + 4]

        on_core(whole, singles)


def pack(slot_block, loaded, keep, given):
    return local_call(
        pack_kernel,
        "pack_states",
        jax.ShapeDtypeStruct(loaded.shape, loaded.dtype),
        [SCALARS] + [WHOLE] * 3,
        input_output_aliases={1: 0},
    )(slot_block, loaded, keep, given)


def total_of(received, *at):
    return jnp.sum(received[(slice(None), *at)].astype(jnp.float32), axis=0)


def relay_kernel(received, out):
    units = received.shape[1] - GROUP
    span = units // GROUP
    for then in EIGHT:
        for unit in range(span):
            total = total_of(received, then * span + unit)
            out[then, unit] = total.astype(jnp.bfloat16)

    def whole():
        for source in EIGHT:
            for i in range(2):
                rows = received[source, units + i]
                for then in EIGHT:
                    out[then, span + 2 * source + i] = rows

    def singles():
        for source in EIGHT:
            for then in EIGHT:
                out[then, span + source] = received[source, units + then]

    on_core(whole, singles)


def relay(received):
    span = received.shape[1] // GROUP - 1
    shape = (GROUP, span + 2 * GROUP) + received.shape[2:]
    out = jax.ShapeDtypeStruct(shape, received.dtype)
    return local_call(relay_kernel, "relay", out, [WHOLE])(received)


def sum_kernel(received, copies, state):
    span = received.shape[1] - 2 * GROUP
    total = jnp.concatenate([total_of(received, unit) for unit in range(span)], axis=0)
    total = total.astype(jnp.bfloat16)
    for peer in range(copies.shape[0]):
        copies[peer] = total

    def whole():
        for later in EIGHT:
            for early in EIGHT:
                for i in range(2):
                    state[PLACE[early, later], i] = received[later, span + 2 * early + i]

    def singles():
        for later in EIGHT:
            for early in EIGHT:
                state[PLACE[later, early], 0] = received[later, span + early]

    on_core(whole, singles)


def sum_terms(received):
    rows, width = received.shape[2:]
    span = received.shape[1] - 2 * GROUP
    outs = [
        jax.ShapeDtypeStruct((GROUP, span * rows, width), received.dtype),
        jax.ShapeDtypeStruct((GROUP * GROUP, 2, rows, width), received.dtype),
    ]
    return local_call(sum_kernel, "sum_terms", outs, [WHOLE])(received)


def shards(
    grad_parts,
    slot_block,
    gram_left,
    gram_right,
    left_basis_t,
    right_basis,
    moment_first,
    moment_second,
):
    blocks = grad_parts.shape[1]
    q_total = grad_parts.shape[2]
    half_span = grad_parts.shape[3]
    width = grad_parts.shape[4]
    core = lax.axis_index("fsdp")

    states = (left_basis_t, right_basis, moment_first, moment_second)
    states = tuple(in_hbm(part) for part in states)
    terms = grad_parts[0].reshape(blocks, GROUP, q_total // GROUP, half_span, width)
    keep, give = halves(*states)
    message = pack(in_hbm(slot_block), load(terms), keep, swap_cores(give))
    received = exchange(relay(exchange(message, FIRST)), SECOND)
    raw, half = sum_terms(received)
    raw = exchange(raw, BLOCK).reshape(-1, width)

    given = swap_cores(half)
    right = jnp.where(core == 0, half, given).reshape(width, width)
    singles = jnp.where(core == 0, given, half)[:, 0]
    left_t = singles[:, 0]
    first = singles[:, 1].astype(jnp.float32) + singles[:, 2].astype(jnp.float32)
    second = singles[:, 3].astype(jnp.float32)

    home = chain(raw, swap_cores(raw), right, left_t, first, second)
    home = exchange(home.reshape(blocks * GROUP, 8, width), ALL)

    outs = finish(
        slot_block,
        home.reshape(width, width),
        (gram_left, gram_right, moment_first, moment_second),
    )
    return (*outs[:4], outs[4][:, None])


def solution(mesh):
    state = P("fsdp", "dp", None)
    return jax.shard_map(
        shards,
        mesh=mesh,
        in_specs=(P("dp", None, None, "fsdp", None), P()) + (state,) * 6,
        out_specs=(state,) * 4 + (P(None, "dp", "fsdp", None),),
        check_vma=False,
    )
```

```python
import jax
import jax.numpy as jnp
from jax import lax
from jax.experimental import pallas as pl
from jax.experimental.pallas import tpu as pltpu
from jax.sharding import PartitionSpec as P

shampoo_beta = 0.9
adam_first = 0.95
adam_second = 0.95
epsilon = 1e-08

GROUP = 8
AXES = ("fsdp", "dp")


def number(dp):
    b = g = 0
    for axis in range(3):
        place = (dp >> (2 * axis)) & 3
        wrap, inner = place >> 1, (place ^ (place >> 1)) & 1
        b += (inner if axis == 2 else wrap) << axis
        g += (wrap if axis == 2 else inner) << axis
    return b, g


PLACE = {number(dp): dp for dp in range(GROUP * GROUP)}
EIGHT = range(GROUP)


def device(c, b, g):
    return c * GROUP * GROUP + PLACE[b, g]


OVER_B = [[[device(c, b, g) for b in EIGHT] for g in EIGHT] for c in range(2)]
OVER_G = [[[device(c, b, g) for g in EIGHT] for b in EIGHT] for c in range(2)]
FIRST = OVER_B[0] + OVER_G[1]
SECOND = OVER_G[0] + OVER_B[1]
BLOCK = OVER_G[0] + OVER_G[1]
ALL = [[device(c, b, g) for b in EIGHT for g in EIGHT] for c in range(2)]


def exchange(x, groups):
    return lax.all_to_all(x, AXES, 0, 0, axis_index_groups=groups, tiled=True)


def swap_cores(x):
    return lax.ppermute(x, "fsdp", [(0, 1), (1, 0)])


def dot(a, b, ca=1, cb=0):
    return lax.dot_general(a, b, (((ca,), (cb,)), ((), ())), preferred_element_type=jnp.float32)


def iota(shape, axis):
    return lax.broadcasted_iota(jnp.int32, shape, axis)


def one_hot(hit):
    return jnp.where(hit, 1.0, 0.0).astype(jnp.bfloat16)


WHOLE = pl.BlockSpec(memory_space=pltpu.VMEM)
SCALARS = pl.BlockSpec(memory_space=pltpu.SMEM)
FAR = pl.BlockSpec(memory_space=pltpu.HBM)


def in_hbm(x):
    return pltpu.with_memory_space_constraint(x, pltpu.HBM)


def local_call(kernel, name, out_shape, in_specs, scratch=(), out=WHOLE, **options):
    return pl.pallas_call(
        kernel,
        out_shape=out_shape,
        in_specs=in_specs,
        out_specs=jax.tree.map(lambda _: out, out_shape),
        scratch_shapes=list(scratch),
        compiler_params=pltpu.CompilerParams(vmem_limit_bytes=40 * 2**20),
        name=name,
        **options,
    )


def chain_kernel(raw, swapped, right, left_t, first, second, out):
    bf16 = jnp.bfloat16
    core = lax.axis_index("fsdp")
    lane = number(lax.axis_index("dp"))[1]
    size = raw.shape[1]
    picks = size // 8

    n = iota((256, 256), 0)
    at = ((n >> 2) & 1) * 128 + (n >> 6) * 32 + ((n >> 3) & 7) * 4 + (n & 3)
    pick = one_hot(iota((256, 256), 1) == at)
    low = jnp.where(core == 0, raw[...], swapped[...])
    high = jnp.where(core == 0, swapped[...], raw[...])
    block = []
    for i in range(0, size // 2, 128):
        rows = jnp.concatenate([low[i : i + 128], high[i : i + 128]], axis=0)
        block.append(dot(pick, rows).astype(bf16))
    block = jnp.concatenate(block, axis=0)

    half_rot = dot(left_t[...], block).astype(bf16)
    rotated = dot(half_rot, right[...])
    new_first = adam_first * first[...] + (1.0 - adam_first) * rotated
    new_second = adam_second * second[...] + (1.0 - adam_second) * rotated * rotated
    scaled = (new_first / (jnp.sqrt(new_second) + epsilon)).astype(bf16)
    back = dot(scaled, right[...], 1, 1).astype(bf16)
    update = dot(left_t[...], back, 0, 0)

    own = one_hot(iota((picks, size), 1) == iota((picks, size), 0) * 8 + lane)
    gram_l = dot(dot(own, block).astype(bf16), block, 1, 1).astype(bf16)
    gram_r = dot(dot(block, own, 1, 1).astype(bf16), block, 0, 0).astype(bf16)

    upper = rotated.astype(bf16)
    lower = (rotated - upper.astype(jnp.float32)).astype(bf16)
    rows = jnp.concatenate([gram_l, gram_r, upper, lower], axis=0)
    n, col = iota((size, 4 * picks), 0), iota((size, 4 * picks), 1)
    spread = one_hot(col == ((n & 7) - 4 * (1 - core)) * picks + (n >> 3))
    kept = (iota((size, size), 0) & 4) == 4 * core
    result = jnp.where(kept, update, dot(spread, rows))
    order = [PLACE[b, g] * 8 for b in EIGHT for g in EIGHT]
    out[...] = jnp.concatenate([result[at : at + 8] for at in order], axis=0).astype(bf16)


def chain(raw, *others):
    width = raw.shape[1]
    out = jax.ShapeDtypeStruct((width, width), jnp.bfloat16)
    return local_call(chain_kernel, "block_chain", out, [WHOLE] * 6)(raw, *others)


def finish_kernel(slot_block, home, gram_l, gram_r, first, second, *refs):
    outs, built, sent = refs[:5], refs[5:10], refs[10]
    core = lax.axis_index("fsdp")
    blocks = home.shape[0]
    n, col = iota((32, 64), 0), iota((32, 64), 1)
    kind, chip, row = n >> 3, col >> 3, col & 7
    other = row - 4 * (1 - core)
    product = (chip == (n & 7)) & ((other == kind) | ((kind == 2) & (other == 3)))
    hit = ((kind == 3) & (row - 4 * core == (n & 7))) | ((kind < 3) & product)
    take = one_hot(hit)
    share = jnp.where(slot_block[core, 0] >= 0, 1.0, 0.0)
    copies = []
    for slot in range(blocks):
        block = jnp.maximum(slot_block[core, slot], 0)
        rows = dot(take, home[block]) * share
        rotated = rows[16:24]
        built[0][slot] = shampoo_beta * gram_l[slot] + (1.0 - shampoo_beta) * rows[:8]
        built[1][slot] = shampoo_beta * gram_r[slot] + (1.0 - shampoo_beta) * rows[8:16]
        built[2][slot] = adam_first * first[slot] + (1.0 - adam_first) * rotated
        built[3][slot] = (
            adam_second * second[slot] + (1.0 - adam_second) * rotated * rotated
        )
        if slot % 4 == 3:
            part = pl.ds(slot - 3, 4)
            for i in range(4):
                copies.append(
                    pltpu.make_async_copy(
                        built[i].at[part], outs[i].at[part], sent.at[i, slot // 4]
                    )
                )
                copies[-1].start()
    for b in range(blocks):
        built[4][b] = dot(take[24:], home[b])[:4].astype(jnp.bfloat16)
    copies.append(pltpu.make_async_copy(built[4], outs[4], sent.at[4, 0]))
    copies[-1].start()
    for copy in copies:
        copy.wait()


def finish(slot_block, home, states):
    blocks, width = home.shape[0], home.shape[2]
    outs = [jax.ShapeDtypeStruct(x.shape, x.dtype) for x in states]
    outs.append(jax.ShapeDtypeStruct((blocks, 4, width), jnp.bfloat16))
    return local_call(
        finish_kernel,
        "new_state",
        outs,
        [SCALARS] + [WHOLE] * 5,
        [pltpu.VMEM(x.shape, x.dtype) for x in outs] + [pltpu.SemaphoreType.DMA((5, 2))],
        out=FAR,
    )(slot_block, home, *states)


def on_core(zero, one):
    core = lax.axis_index("fsdp")
    pl.when(core == 0)(zero)
    pl.when(core != 0)(one)


def halves_kernel(left_t, right, first, second, keep, give, *scratch):
    held, done = scratch[:4], scratch[4]
    copies = [
        pltpu.make_async_copy(source, to, done.at[i])
        for i, (source, to) in enumerate(zip((left_t, right, first, second), held))
    ]
    for copy in copies:
        copy.start()
    for copy in copies:
        copy.wait()
    core = lax.axis_index("fsdp")
    for slot in range(keep.shape[0]):
        left_rows, right_rows, one, two = (part[slot].astype(jnp.float32) for part in held)
        upper = one.astype(jnp.bfloat16).astype(jnp.float32)
        whole = jnp.concatenate([right_rows] * 4, axis=0)
        singles = jnp.concatenate([left_rows, upper, one - upper, two], axis=0)
        keep[slot] = jnp.where(core == 0, whole, singles).astype(jnp.bfloat16)
        give[slot] = jnp.where(core == 0, singles, whole).astype(jnp.bfloat16)


def halves(*states):
    blocks, rows, width = states[0].shape
    return local_call(
        halves_kernel,
        "state_halves",
        [jax.ShapeDtypeStruct((blocks, 4 * rows, width), jnp.bfloat16)] * 2,
        [FAR] * 4,
        [pltpu.VMEM(x.shape, x.dtype) for x in states] + [pltpu.SemaphoreType.DMA((4,))],
    )(*states)


def load_kernel(terms, by_block, out, done):
    blocks, chips, span = terms.shape[:3]
    near = [
        pltpu.make_async_copy(by_block.at[b], out.at[b, pl.ds(0, chips * span)], done.at[b])
        for b in range(blocks)
    ]
    cross = [
        pltpu.make_async_copy(terms.at[b], out.at[:, pl.ds(b * span, span)], done.at[b])
        for b in range(blocks)
    ]
    for b in range(blocks):
        on_core(near[b].start, cross[b].start)
    for b in range(blocks):
        on_core(near[b].wait, cross[b].wait)


def load(terms):
    blocks, chips, span, rows, width = terms.shape
    return local_call(
        load_kernel,
        "load_terms",
        jax.ShapeDtypeStruct((blocks, chips * span + GROUP, rows, width), terms.dtype),
        [FAR] * 2,
        [pltpu.SemaphoreType.DMA((blocks,))],
        cost_estimate=pl.CostEstimate(flops=0, bytes_accessed=2 * terms.nbytes, transcendentals=0),
    )(in_hbm(terms), in_hbm(terms.reshape(blocks, chips * span, rows, width)))


def pack_kernel(slot_block, loaded, keep, given, out):
    core = lax.axis_index("fsdp")
    blocks = out.shape[0]
    units = out.shape[1] - GROUP
    mine = slot_block[core, 0] >= 0
    state = []
    for b in range(blocks):
        at = 0
        for owner in range(slot_block.shape[0]):
            for slot in range(blocks):
                at += jnp.where(slot_block[owner, slot] == b, slot, 0)
        state.append(jnp.where(mine, keep[at], given[at]))

    def whole():
        for b in range(blocks):
            right = state[b][:8].astype(jnp.float32)
            out[b, units] = right[:4].astype(jnp.bfloat16)
            out[b, units + 1] = right[4:].astype(jnp.bfloat16)

    def singles():
        size = 32 * blocks
        n, col = iota((size, size), 0), iota((size, size), 1)
        turn = one_hot(col == (n & ~31) + (n & 3) * 8 + ((n >> 2) & 7))
        turned = dot(turn, jnp.concatenate(state, axis=0)).astype(jnp.bfloat16)
        for b in range(blocks):
            for g in EIGHT:
                at = 32 * b + 4 * g
                out[g, units + b] = turned[at : at + 4]

    on_core(whole, singles)


def pack(slot_block, loaded, keep, given):
    return local_call(
        pack_kernel,
        "pack_states",
        jax.ShapeDtypeStruct(loaded.shape, loaded.dtype),
        [SCALARS] + [WHOLE] * 3,
        input_output_aliases={1: 0},
    )(slot_block, loaded, keep, given)


def total_of(received, *at):
    return jnp.sum(received[(slice(None), *at)].astype(jnp.float32), axis=0)


def relay_kernel(received, out):
    units = received.shape[1] - GROUP
    span = units // GROUP
    for then in EIGHT:
        for unit in range(span):
            total = total_of(received, then * span + unit)
            out[then, unit] = total.astype(jnp.bfloat16)

    def whole():
        for source in EIGHT:
            for i in range(2):
                rows = received[source, units + i]
                for then in EIGHT:
                    out[then, span + 2 * source + i] = rows

    def singles():
        for source in EIGHT:
            for then in EIGHT:
                out[then, span + source] = received[source, units + then]

    on_core(whole, singles)


def relay(received):
    span = received.shape[1] // GROUP - 1
    shape = (GROUP, span + 2 * GROUP) + received.shape[2:]
    out = jax.ShapeDtypeStruct(shape, received.dtype)
    return local_call(relay_kernel, "relay", out, [WHOLE])(received)


def sum_kernel(received, copies, state):
    span = received.shape[1] - 2 * GROUP
    total = jnp.concatenate([total_of(received, unit) for unit in range(span)], axis=0)
    total = total.astype(jnp.bfloat16)
    for peer in range(copies.shape[0]):
        copies[peer] = total

    def whole():
        for later in EIGHT:
            for early in EIGHT:
                for i in range(2):
                    state[PLACE[early, later], i] = received[later, span + 2 * early + i]

    def singles():
        for later in EIGHT:
            for early in EIGHT:
                state[PLACE[later, early], 0] = received[later, span + early]

    on_core(whole, singles)


def sum_terms(received):
    rows, width = received.shape[2:]
    span = received.shape[1] - 2 * GROUP
    outs = [
        jax.ShapeDtypeStruct((GROUP, span * rows, width), received.dtype),
        jax.ShapeDtypeStruct((GROUP * GROUP, 2, rows, width), received.dtype),
    ]
    return local_call(sum_kernel, "sum_terms", outs, [WHOLE])(received)


def shards(
    grad_parts,
    slot_block,
    gram_left,
    gram_right,
    left_basis_t,
    right_basis,
    moment_first,
    moment_second,
):
    blocks = grad_parts.shape[1]
    q_total = grad_parts.shape[2]
    half_span = grad_parts.shape[3]
    width = grad_parts.shape[4]
    core = lax.axis_index("fsdp")

    states = (left_basis_t, right_basis, moment_first, moment_second)
    states = tuple(in_hbm(part) for part in states)
    terms = grad_parts[0].reshape(blocks, GROUP, q_total // GROUP, half_span, width)
    keep, give = halves(*states)
    message = pack(in_hbm(slot_block), load(terms), keep, swap_cores(give))
    received = exchange(relay(exchange(message, FIRST)), SECOND)
    raw, half = sum_terms(received)
    raw = exchange(raw, BLOCK).reshape(-1, width)

    given = swap_cores(half)
    right = jnp.where(core == 0, half, given).reshape(width, width)
    singles = jnp.where(core == 0, given, half)[:, 0]
    left_t = singles[:, 0]
    first = singles[:, 1].astype(jnp.float32) + singles[:, 2].astype(jnp.float32)
    second = singles[:, 3].astype(jnp.float32)

    home = chain(raw, swap_cores(raw), right, left_t, first, second)
    home = exchange(home.reshape(blocks * GROUP, 8, width), ALL)

    outs = finish(
        slot_block,
        home.reshape(blocks, GROUP * 8, width),
        (gram_left, gram_right, moment_first, moment_second),
    )
    return (*outs[:4], outs[4][:, None])


def solution(mesh):
    state = P("fsdp", "dp", None)
    return jax.shard_map(
        shards,
        mesh=mesh,
        in_specs=(P("dp", None, None, "fsdp", None), P()) + (state,) * 6,
        out_specs=(state,) * 4 + (P(None, "dp", "fsdp", None),),
        check_vma=False,
    )
```

```python
import jax
import jax.numpy as jnp
from jax import lax
from jax.experimental import pallas as pl
from jax.experimental.pallas import tpu as pltpu
from jax.sharding import PartitionSpec as P

shampoo_beta = 0.9
adam_first = 0.95
adam_second = 0.95
epsilon = 1e-08

GROUP = 8
AXES = ("fsdp", "dp")


def number(dp):
    b = g = 0
    for axis in range(3):
        place = (dp >> (2 * axis)) & 3
        b += (place >> 1) << axis
        g += ((place ^ (place >> 1)) & 1) << axis
    return b, g


PLACE = {number(dp): dp for dp in range(GROUP * GROUP)}
EIGHT = range(GROUP)


def device(c, b, g):
    return c * GROUP * GROUP + PLACE[b, g]


OVER_B = [[[device(c, b, g) for b in EIGHT] for g in EIGHT] for c in range(2)]
OVER_G = [[[device(c, b, g) for g in EIGHT] for b in EIGHT] for c in range(2)]
FIRST = OVER_B[0] + OVER_G[1]
SECOND = OVER_G[0] + OVER_B[1]
BLOCK = OVER_G[0] + OVER_G[1]
ALL = [[device(c, b, g) for b in EIGHT for g in EIGHT] for c in range(2)]


def exchange(x, groups):
    return lax.all_to_all(x, AXES, 0, 0, axis_index_groups=groups, tiled=True)


def swap_cores(x):
    return lax.ppermute(x, "fsdp", [(0, 1), (1, 0)])


def dot(a, b, ca=1, cb=0):
    return lax.dot_general(a, b, (((ca,), (cb,)), ((), ())), preferred_element_type=jnp.float32)


def iota(shape, axis):
    return lax.broadcasted_iota(jnp.int32, shape, axis)


def one_hot(hit):
    return jnp.where(hit, 1.0, 0.0).astype(jnp.bfloat16)


WHOLE = pl.BlockSpec(memory_space=pltpu.VMEM)
SCALARS = pl.BlockSpec(memory_space=pltpu.SMEM)
FAR = pl.BlockSpec(memory_space=pltpu.HBM)


def in_hbm(x):
    return pltpu.with_memory_space_constraint(x, pltpu.HBM)


def local_call(kernel, name, out_shape, in_specs, scratch=(), out=WHOLE, **options):
    return pl.pallas_call(
        kernel,
        out_shape=out_shape,
        in_specs=in_specs,
        out_specs=jax.tree.map(lambda _: out, out_shape),
        scratch_shapes=list(scratch),
        compiler_params=pltpu.CompilerParams(vmem_limit_bytes=40 * 2**20),
        name=name,
        **options,
    )


def chain_kernel(raw, swapped, right, left_t, first, second, out):
    bf16 = jnp.bfloat16
    core = lax.axis_index("fsdp")
    lane = number(lax.axis_index("dp"))[1]
    size = raw.shape[1]
    picks = size // 8

    n = iota((256, 256), 0)
    at = ((n >> 2) & 1) * 128 + (n >> 6) * 32 + ((n >> 3) & 7) * 4 + (n & 3)
    pick = one_hot(iota((256, 256), 1) == at)
    low = jnp.where(core == 0, raw[...], swapped[...])
    high = jnp.where(core == 0, swapped[...], raw[...])
    block = []
    for i in range(0, size // 2, 128):
        rows = jnp.concatenate([low[i : i + 128], high[i : i + 128]], axis=0)
        block.append(dot(pick, rows).astype(bf16))
    block = jnp.concatenate(block, axis=0)

    half_rot = dot(left_t[...], block).astype(bf16)
    rotated = dot(half_rot, right[...])
    new_first = adam_first * first[...] + (1.0 - adam_first) * rotated
    new_second = adam_second * second[...] + (1.0 - adam_second) * rotated * rotated
    scaled = (new_first / (jnp.sqrt(new_second) + epsilon)).astype(bf16)
    back = dot(scaled, right[...], 1, 1).astype(bf16)
    update = dot(left_t[...], back, 0, 0)

    own = one_hot(iota((picks, size), 1) == iota((picks, size), 0) * 8 + lane)
    gram_l = dot(dot(own, block).astype(bf16), block, 1, 1).astype(bf16)
    gram_r = dot(dot(block, own, 1, 1).astype(bf16), block, 0, 0).astype(bf16)

    upper = rotated.astype(bf16)
    lower = (rotated - upper.astype(jnp.float32)).astype(bf16)
    rows = jnp.concatenate([gram_l, gram_r, upper, lower], axis=0)
    n, col = iota((size, 4 * picks), 0), iota((size, 4 * picks), 1)
    spread = one_hot(col == ((n & 7) - 4 * (1 - core)) * picks + (n >> 3))
    kept = (iota((size, size), 0) & 4) == 4 * core
    result = jnp.where(kept, update, dot(spread, rows))
    order = [PLACE[b, g] * 8 for b in EIGHT for g in EIGHT]
    out[...] = jnp.concatenate([result[at : at + 8] for at in order], axis=0).astype(bf16)


def chain(raw, *others):
    width = raw.shape[1]
    out = jax.ShapeDtypeStruct((width, width), jnp.bfloat16)
    return local_call(chain_kernel, "block_chain", out, [WHOLE] * 6)(raw, *others)


def finish_kernel(slot_block, home, gram_l, gram_r, first, second, *refs):
    outs, built, sent = refs[:5], refs[5:10], refs[10]
    core = lax.axis_index("fsdp")
    blocks = home.shape[0]
    n, col = iota((32, 64), 0), iota((32, 64), 1)
    kind, chip, row = n >> 3, col >> 3, col & 7
    other = row - 4 * (1 - core)
    product = (chip == (n & 7)) & ((other == kind) | ((kind == 2) & (other == 3)))
    hit = ((kind == 3) & (row - 4 * core == (n & 7))) | ((kind < 3) & product)
    take = one_hot(hit)
    share = jnp.where(slot_block[core, 0] >= 0, 1.0, 0.0)
    copies = []
    for slot in range(blocks):
        block = jnp.maximum(slot_block[core, slot], 0)
        rows = dot(take, home[block]) * share
        rotated = rows[16:24]
        built[0][slot] = shampoo_beta * gram_l[slot] + (1.0 - shampoo_beta) * rows[:8]
        built[1][slot] = shampoo_beta * gram_r[slot] + (1.0 - shampoo_beta) * rows[8:16]
        built[2][slot] = adam_first * first[slot] + (1.0 - adam_first) * rotated
        built[3][slot] = (
            adam_second * second[slot] + (1.0 - adam_second) * rotated * rotated
        )
        if slot % 4 == 3:
            part = pl.ds(slot - 3, 4)
            for i in range(4):
                copies.append(
                    pltpu.make_async_copy(
                        built[i].at[part], outs[i].at[part], sent.at[i, slot // 4]
                    )
                )
                copies[-1].start()
    for b in range(blocks):
        built[4][b] = dot(take[24:], home[b])[:4].astype(jnp.bfloat16)
    copies.append(pltpu.make_async_copy(built[4], outs[4], sent.at[4, 0]))
    copies[-1].start()
    for copy in copies:
        copy.wait()


def finish(slot_block, home, states):
    blocks, width = home.shape[0], home.shape[2]
    outs = [jax.ShapeDtypeStruct(x.shape, x.dtype) for x in states]
    outs.append(jax.ShapeDtypeStruct((blocks, 4, width), jnp.bfloat16))
    return local_call(
        finish_kernel,
        "new_state",
        outs,
        [SCALARS] + [WHOLE] * 5,
        [pltpu.VMEM(x.shape, x.dtype) for x in outs] + [pltpu.SemaphoreType.DMA((5, 2))],
        out=FAR,
    )(slot_block, home, *states)


def on_core(zero, one):
    core = lax.axis_index("fsdp")
    pl.when(core == 0)(zero)
    pl.when(core != 0)(one)


def halves_kernel(left_t, right, first, second, keep, give, *scratch):
    held, done = scratch[:4], scratch[4]
    copies = [
        pltpu.make_async_copy(source, to, done.at[i])
        for i, (source, to) in enumerate(zip((left_t, right, first, second), held))
    ]
    for copy in copies:
        copy.start()
    for copy in copies:
        copy.wait()
    core = lax.axis_index("fsdp")
    for slot in range(keep.shape[0]):
        left_rows, right_rows, one, two = (part[slot].astype(jnp.float32) for part in held)
        upper = one.astype(jnp.bfloat16).astype(jnp.float32)
        whole = jnp.concatenate([right_rows] * 4, axis=0)
        singles = jnp.concatenate([left_rows, upper, one - upper, two], axis=0)
        keep[slot] = jnp.where(core == 0, whole, singles).astype(jnp.bfloat16)
        give[slot] = jnp.where(core == 0, singles, whole).astype(jnp.bfloat16)


def halves(*states):
    blocks, rows, width = states[0].shape
    return local_call(
        halves_kernel,
        "state_halves",
        [jax.ShapeDtypeStruct((blocks, 4 * rows, width), jnp.bfloat16)] * 2,
        [FAR] * 4,
        [pltpu.VMEM(x.shape, x.dtype) for x in states] + [pltpu.SemaphoreType.DMA((4,))],
    )(*states)


def load_kernel(terms, by_block, out, done):
    blocks, chips, span = terms.shape[:3]
    near = [
        pltpu.make_async_copy(by_block.at[b], out.at[b, pl.ds(0, chips * span)], done.at[b])
        for b in range(blocks)
    ]
    cross = [
        pltpu.make_async_copy(terms.at[b], out.at[:, pl.ds(b * span, span)], done.at[b])
        for b in range(blocks)
    ]
    for b in range(blocks):
        on_core(near[b].start, cross[b].start)
    for b in range(blocks):
        on_core(near[b].wait, cross[b].wait)


def load(terms):
    blocks, chips, span, rows, width = terms.shape
    return local_call(
        load_kernel,
        "load_terms",
        jax.ShapeDtypeStruct((blocks, chips * span + GROUP, rows, width), terms.dtype),
        [FAR] * 2,
        [pltpu.SemaphoreType.DMA((blocks,))],
        cost_estimate=pl.CostEstimate(flops=0, bytes_accessed=2 * terms.nbytes, transcendentals=0),
    )(in_hbm(terms), in_hbm(terms.reshape(blocks, chips * span, rows, width)))


def pack_kernel(slot_block, loaded, keep, given, out):
    core = lax.axis_index("fsdp")
    blocks = out.shape[0]
    units = out.shape[1] - GROUP
    mine = slot_block[core, 0] >= 0
    state = []
    for b in range(blocks):
        at = 0
        for owner in range(slot_block.shape[0]):
            for slot in range(blocks):
                at += jnp.where(slot_block[owner, slot] == b, slot, 0)
        state.append(jnp.where(mine, keep[at], given[at]))

    def whole():
        for b in range(blocks):
            right = state[b][:8].astype(jnp.float32)
            out[b, units] = right[:4].astype(jnp.bfloat16)
            out[b, units + 1] = right[4:].astype(jnp.bfloat16)

    def singles():
        size = 32 * blocks
        n, col = iota((size, size), 0), iota((size, size), 1)
        turn = one_hot(col == (n & ~31) + (n & 3) * 8 + ((n >> 2) & 7))
        turned = dot(turn, jnp.concatenate(state, axis=0)).astype(jnp.bfloat16)
        for b in range(blocks):
            for g in EIGHT:
                at = 32 * b + 4 * g
                out[g, units + b] = turned[at : at + 4]

    on_core(whole, singles)


def pack(slot_block, loaded, keep, given):
    return local_call(
        pack_kernel,
        "pack_states",
        jax.ShapeDtypeStruct(loaded.shape, loaded.dtype),
        [SCALARS] + [WHOLE] * 3,
        input_output_aliases={1: 0},
    )(slot_block, loaded, keep, given)


def total_of(received, *at):
    return jnp.sum(received[(slice(None), *at)].astype(jnp.float32), axis=0)


def relay_kernel(received, out):
    units = received.shape[1] - GROUP
    span = units // GROUP
    for then in EIGHT:
        for unit in range(span):
            total = total_of(received, then * span + unit)
            out[then, unit] = total.astype(jnp.bfloat16)

    def whole():
        for source in EIGHT:
            for i in range(2):
                rows = received[source, units + i]
                for then in EIGHT:
                    out[then, span + 2 * source + i] = rows

    def singles():
        for source in EIGHT:
            for then in EIGHT:
                out[then, span + source] = received[source, units + then]

    on_core(whole, singles)


def relay(received):
    span = received.shape[1] // GROUP - 1
    shape = (GROUP, span + 2 * GROUP) + received.shape[2:]
    out = jax.ShapeDtypeStruct(shape, received.dtype)
    return local_call(relay_kernel, "relay", out, [WHOLE])(received)


def sum_kernel(received, copies, state):
    span = received.shape[1] - 2 * GROUP
    total = jnp.concatenate([total_of(received, unit) for unit in range(span)], axis=0)
    total = total.astype(jnp.bfloat16)
    for peer in range(copies.shape[0]):
        copies[peer] = total

    def whole():
        for later in EIGHT:
            for early in EIGHT:
                for i in range(2):
                    state[PLACE[early, later], i] = received[later, span + 2 * early + i]

    def singles():
        for later in EIGHT:
            for early in EIGHT:
                state[PLACE[later, early], 0] = received[later, span + early]

    on_core(whole, singles)


def sum_terms(received):
    rows, width = received.shape[2:]
    span = received.shape[1] - 2 * GROUP
    outs = [
        jax.ShapeDtypeStruct((GROUP, span * rows, width), received.dtype),
        jax.ShapeDtypeStruct((GROUP * GROUP, 2, rows, width), received.dtype),
    ]
    return local_call(sum_kernel, "sum_terms", outs, [WHOLE])(received)


def shards(
    grad_parts,
    slot_block,
    gram_left,
    gram_right,
    left_basis_t,
    right_basis,
    moment_first,
    moment_second,
):
    blocks = grad_parts.shape[1]
    q_total = grad_parts.shape[2]
    half_span = grad_parts.shape[3]
    width = grad_parts.shape[4]
    core = lax.axis_index("fsdp")

    states = (left_basis_t, right_basis, moment_first, moment_second)
    states = tuple(in_hbm(part) for part in states)
    terms = grad_parts[0].reshape(blocks, GROUP, q_total // GROUP, half_span, width)
    keep, give = halves(*states)
    message = pack(in_hbm(slot_block), load(terms), keep, swap_cores(give))
    received = exchange(relay(exchange(message, FIRST)), SECOND)
    raw, half = sum_terms(received)
    raw = exchange(raw, BLOCK).reshape(-1, width)

    given = swap_cores(half)
    right = jnp.where(core == 0, half, given).reshape(width, width)
    singles = jnp.where(core == 0, given, half)[:, 0]
    left_t = singles[:, 0]
    first = singles[:, 1].astype(jnp.float32) + singles[:, 2].astype(jnp.float32)
    second = singles[:, 3].astype(jnp.float32)

    home = chain(raw, swap_cores(raw), right, left_t, first, second)
    home = exchange(home.reshape(blocks * GROUP, 8, width), ALL)

    outs = finish(
        slot_block,
        home.reshape(blocks, GROUP * 8, width),
        (gram_left, gram_right, moment_first, moment_second),
    )
    return (*outs[:4], outs[4][:, None])


def solution(mesh):
    state = P("fsdp", "dp", None)
    return jax.shard_map(
        shards,
        mesh=mesh,
        in_specs=(P("dp", None, None, "fsdp", None), P()) + (state,) * 6,
        out_specs=(state,) * 4 + (P(None, "dp", "fsdp", None),),
        check_vma=False,
    )
```
